32 devices in a mesh: depth: 4 (over y, x), row: 2 (over core), col: 4 (over z).
Axes of the slice: x: 2, y: 2, z: 4, core: 2. Of those that a mesh axis runs over, the one named last changes fastest.
Arguments:
- tokens: float32 [1024, 8192], P(('depth', 'col'), 'row'), may hold values from -16 to 16
- w_query: float32 [8192, 4096], P('row', 'col'), may hold values from -0.0625 to 0.0625
- w_key: float32 [8192, 512], P('row', 'col'), may hold values from -0.0625 to 0.0625
- w_value: float32 [8192, 512], P('row', 'col'), may hold values from -0.0625 to 0.0625
- w_out: float32 [4096, 8192], P('col', 'row'), may hold values from -0.09375 to 0.09375
Outputs:
- mixed: float32 [1024, 8192], P(('depth', 'col'), 'row')
The draws below stay inside these ranges and needn't reach their ends.
All inputs are finite; a program needn't handle non-finite values.
Results may differ from the reference program's by a relative error of at most 0.0003.
Values sent between devices are 32-bit elements; how exact they have to be, the bound alone decides.
No kernel may reach another device: no remote copies, remote signals or barrier semaphores. Data moves between devices by JAX's collectives and lax.ppermute only.
A program may use at most 128 MiB of HBM per device.

```python
import math
import jax
import jax.numpy as jnp
from jax import lax

D = 8192
QUERY_HEADS = 32
KEY_VALUE_HEADS = 4
HEAD_SIZE_DIM = 128
TOKENS_PER_SET = 256
TOKEN_TOTAL = 1024
QUERY_WIDTH = 4096
KW = 512
N_DEPTH = 4


def draw_tokens(key, part):
    normal_part = jnp.clip(jax.random.normal(key, (TOKEN_TOTAL, D), jnp.float32), -5.0, 5.0)
    return normal_part


def steps_of(key, extent, split, low, largest):
    def one(position, blocks):
        heights = jax.random.uniform(jax.random.fold_in(jax.random.fold_in(key, 6), position), (blocks,), jnp.float32, low / len(split), largest / len(split))
        return jnp.repeat(jnp.exp(heights), extent[position] // blocks).reshape((-1,) + (1,) * (len(extent) - position - 1))

    level = one(*split[0])
    for cut in split[1:]:
        level = level * one(*cut)
    return level


def centred(rng, extent, scale, reach, cuts=(), held_as=jnp.bfloat16):
    array = jax.random.normal(rng, extent, jnp.float32) * scale
    if len(cuts) > 0:
        array = steps_of(rng, extent, cuts, -0.22, 0.18) * array
    return jnp.clip(array, min=-reach, max=reach).astype(held_as)


def setup_inputs(seed: int = 0) -> dict:
    arg_keys = jax.random.split(jax.random.key(seed), 6)
    return {
        "tokens": draw_tokens(jax.random.fold_in(arg_keys[5], 71), 0),
        "w_query": centred(arg_keys[1], (D, QUERY_WIDTH), D ** -0.5, 0.0625, ((0, 2), (1, 4)), jnp.float32),
        "w_key": centred(arg_keys[2], (D, KW), D ** -0.5, 0.0625, ((0, 2), (1, 4)), jnp.float32),
        "w_value": centred(arg_keys[3], (D, KW), D ** -0.5, 0.0625, ((0, 2), (1, 4)), jnp.float32),
        "w_out": centred(arg_keys[4], (QUERY_WIDTH, D), QUERY_WIDTH ** -0.5, 0.09375, ((0, 4), (1, 2)), jnp.float32),
    }


def reference(tokens, w_query, w_key, w_value, w_out):
    highest = lax.Precision.HIGHEST
    query_rows = jnp.dot(tokens, w_query, preferred_element_type=jnp.float32, precision=highest)
    key_rows = jnp.dot(tokens, w_key, preferred_element_type=jnp.float32, precision=highest)
    value_rows = jnp.dot(tokens, w_value, preferred_element_type=jnp.float32, precision=highest)
    queries_per_group = QUERY_HEADS // KEY_VALUE_HEADS
    score_scale = 1.0 / math.sqrt(HEAD_SIZE_DIM)
    query_head_rows = query_rows.reshape(N_DEPTH, TOKENS_PER_SET, KEY_VALUE_HEADS, queries_per_group, HEAD_SIZE_DIM).transpose(0, 2, 1, 3, 4).reshape(N_DEPTH * KEY_VALUE_HEADS, TOKENS_PER_SET, queries_per_group, HEAD_SIZE_DIM)
    key_head_rows = key_rows.reshape(N_DEPTH, TOKENS_PER_SET, KEY_VALUE_HEADS, HEAD_SIZE_DIM).transpose(0, 2, 1, 3).reshape(N_DEPTH * KEY_VALUE_HEADS, TOKENS_PER_SET, HEAD_SIZE_DIM)
    value_head_rows = value_rows.reshape(N_DEPTH, TOKENS_PER_SET, KEY_VALUE_HEADS, HEAD_SIZE_DIM).transpose(0, 2, 1, 3).reshape(N_DEPTH * KEY_VALUE_HEADS, TOKENS_PER_SET, HEAD_SIZE_DIM)

    def one_group(triple):
        head_query, head_key, head_value = triple
        scores = jnp.einsum('tgd,sd->gts', head_query, head_key, precision=highest) * score_scale
        weights = jax.nn.softmax(scores, axis=-1)
        return jnp.einsum('gts,sd->tgd', weights, head_value, precision=highest)
    attention_output = lax.map(one_group, (query_head_rows, key_head_rows, value_head_rows))
    attention_output = attention_output.reshape(N_DEPTH, KEY_VALUE_HEADS, TOKENS_PER_SET, queries_per_group, HEAD_SIZE_DIM).transpose(0, 2, 1, 3, 4).reshape(TOKEN_TOTAL, QUERY_WIDTH)
    return jnp.dot(attention_output, w_out, preferred_element_type=jnp.float32, precision=highest)
```

```python
import functools
import math

import jax
import jax.numpy as jnp
from jax import lax
from jax.experimental import pallas as pl
from jax.experimental.pallas import tpu as pltpu
from jax.sharding import PartitionSpec as P

QUERY_HEADS = 32
KEY_VALUE_HEADS = 4
HEAD_SIZE_DIM = 128
GROUP = QUERY_HEADS // KEY_VALUE_HEADS

VMEM_LIMIT = 40 * 1024 * 1024

ENDS_IN = [(1, 0), (2, 3)]
ENDS_OUT = [(0, 1), (3, 2)]
PAIRS = [(0, 1), (1, 0), (2, 3), (3, 2)]
MIDDLE = [(1, 2), (2, 1)]
CORES = [(0, 1), (1, 0)]


def split(a):
    high = a.astype(jnp.bfloat16)
    return high, (a - high.astype(jnp.float32)).astype(jnp.bfloat16)


def dot(a, b, dims=((1,), (0,))):
    return lax.dot_general(a, b, (dims, ((), ())), preferred_element_type=jnp.float32)


def dot3(a, b, dims=((1,), (0,))):
    rows = a[0].shape[0]
    both = dot(jnp.concatenate(a, axis=0), b[0], dims)
    return both[:rows] + (both[rows:] + dot(a[0], b[1], dims))


def project_kernel(terms, with_total, *refs):
    n_x = sum(terms)
    x_refs, (wq, wk, wv), rest = refs[:n_x], refs[n_x : n_x + 3], refs[n_x + 3 :]
    out = rest[-1]

    @pl.when(pl.program_id(0) == 0)
    def _():
        out[...] = rest[0][...] if with_total else jnp.zeros_like(out)

    blocks, at = [], 0
    for n in terms:
        block = x_refs[at][...]
        for r in x_refs[at + 1 : at + n]:
            block = block + r[...]
        blocks.append(block)
        at += n
    x = split(jnp.concatenate(blocks, axis=0) if len(blocks) > 1 else blocks[0])
    offset = 0
    for w in (wq, wk, wv):
        width = w.shape[1]
        out[:, offset : offset + width] += dot3(x, split(w[...]))
        offset += width


def project(blocks, weights, chunk, total=None, step=512):
    terms = tuple(len(b) for b in blocks)
    flat = [a for b in blocks for a in b]
    depth = flat[0].shape[1]
    rows = sum(b[0].shape[0] for b in blocks)
    steps = depth // step
    width = sum(w.shape[1] for w in weights)
    first = chunk * steps
    in_specs = [pl.BlockSpec((a.shape[0], step), lambda k: (0, k)) for a in flat]
    in_specs += [pl.BlockSpec((step, w.shape[1]), lambda k: (first + k, 0)) for w in weights]
    operands = flat + list(weights)
    if total is not None:
        in_specs.append(pl.BlockSpec((rows, width), lambda k: (0, 0)))
        operands.append(total)
    return pl.pallas_call(
        functools.partial(project_kernel, terms, total is not None),
        grid=(steps,),
        in_specs=in_specs,
        out_specs=pl.BlockSpec((rows, width), lambda k: (0, 0)),
        out_shape=jax.ShapeDtypeStruct((rows, width), jnp.float32),
        compiler_params=pltpu.CompilerParams(vmem_limit_bytes=VMEM_LIMIT),
        cost_estimate=pl.CostEstimate(
            flops=6 * rows * depth * width, bytes_accessed=4 * depth * (rows + width), transcendentals=0
        ),
        name="project",
    )(*operands)


def attend(parts, q_width, kv_width, store):
    groups = kv_width // HEAD_SIZE_DIM
    scale = 1.0 / math.sqrt(HEAD_SIZE_DIM)

    def columns(start, width):
        return jnp.concatenate([a[:, start : start + width] + b[:, start : start + width] for a, b in parts], axis=0)

    for g in range(groups):
        at = q_width + g * HEAD_SIZE_DIM
        keys = split(columns(at, HEAD_SIZE_DIM))
        values = split(columns(at + kv_width, HEAD_SIZE_DIM))
        for j in range(GROUP):
            head = (g * GROUP + j) * HEAD_SIZE_DIM
            queries = split(columns(head, HEAD_SIZE_DIM) * scale)
            scores = dot3(queries, keys, ((1,), (1,)))
            weights = jnp.exp(scores - jnp.max(scores, axis=-1, keepdims=True))
            total = jnp.sum(weights, axis=-1, keepdims=True)
            store(head, dot3(split(weights), values) / total)


def attend_out_kernel(n_parts, q_width, kv_width, *refs):
    part_refs, w_ref, rest = refs[: 2 * n_parts], refs[2 * n_parts], refs[2 * n_parts + 1 :]
    high, low, outs = rest[0], rest[1], rest[2:]

    @pl.when(pl.program_id(0) == 0)
    def _():
        def store(head, rows):
            h, l = split(rows)
            high[:, head : head + HEAD_SIZE_DIM] = h
            low[:, head : head + HEAD_SIZE_DIM] = l

        attend([(part_refs[2 * i], part_refs[2 * i + 1]) for i in range(n_parts)], q_width, kv_width, store)

    mix(high, low, w_ref, outs)


def mix(high, low, w_ref, outs):
    mixed = dot3((high[...], low[...]), split(w_ref[...]))
    at = 0
    for o in outs:
        o[...] = mixed[at : at + o.shape[0]]
        at += o.shape[0]


def mix_kernel(high, low, w_ref, *outs):
    mix(high, low, w_ref, outs)


def attend_out(parts, w_out, kv_width, slots, columns, step=512):
    rows = sum(a.shape[0] for a, _ in parts)
    q_width = w_out.shape[0]
    flat = [r for pair in parts for r in pair]
    whole = pl.BlockSpec((rows, q_width), lambda n: (0, 0))
    bf16 = jax.ShapeDtypeStruct((rows, q_width), jnp.bfloat16)
    res = pl.pallas_call(
        functools.partial(attend_out_kernel, len(parts), q_width, kv_width),
        grid=(columns // step,),
        in_specs=[pl.BlockSpec(a.shape, lambda n: (0, 0)) for a in flat]
        + [pl.BlockSpec((q_width, step), lambda n: (0, n))],
        out_specs=[whole, whole] + [pl.BlockSpec((s, step), lambda n: (0, n)) for s in slots],
        out_shape=[bf16, bf16] + [jax.ShapeDtypeStruct((s, columns), jnp.float32) for s in slots],
        compiler_params=pltpu.CompilerParams(vmem_limit_bytes=VMEM_LIMIT),
        cost_estimate=pl.CostEstimate(
            flops=6 * rows * q_width * columns + 24 * rows * rows * q_width,
            bytes_accessed=4 * columns * (q_width + rows),
            transcendentals=rows * rows * q_width // HEAD_SIZE_DIM,
        ),
        name="attend_out",
    )(*flat, w_out)
    return res[:2], res[2:]


def out_again(attended, w_out, slots, chunk, columns, step=512):
    high, low = attended
    rows, q_width = high.shape
    first = chunk * columns // step
    whole = pl.BlockSpec((rows, q_width), lambda n: (0, 0))
    return pl.pallas_call(
        mix_kernel,
        grid=(columns // step,),
        in_specs=[whole, whole, pl.BlockSpec((q_width, step), lambda n: (0, first + n))],
        out_specs=[pl.BlockSpec((s, step), lambda n: (0, n)) for s in slots],
        out_shape=[jax.ShapeDtypeStruct((s, columns), jnp.float32) for s in slots],
        compiler_params=pltpu.CompilerParams(vmem_limit_bytes=VMEM_LIMIT),
        cost_estimate=pl.CostEstimate(
            flops=6 * rows * q_width * columns, bytes_accessed=4 * columns * (q_width + rows), transcendentals=0
        ),
        name="out_again",
    )(high, low, w_out)


CHUNKS = 2


def on_line_of_four(tokens, w_query, w_key, w_value, w_out):
    rows, depth = tokens.shape
    weights = (w_query, w_key, w_value)
    kv_width = w_key.shape[1]
    step = depth // CHUNKS

    def hop(a, pairs):
        return lax.ppermute(a, "col", pairs)

    def swap(a):
        return lax.ppermute(a, "row", CORES)

    own = [tokens[:, c * step : (c + 1) * step] for c in range(CHUNKS)]
    near = [hop(a, PAIRS) for a in own]
    mid = [hop(a, MIDDLE) for a in own]
    end2 = [hop(a, ENDS_IN) for a in mid]
    mid2 = [hop(a, MIDDLE) for a in near]
    end3 = [hop(a, ENDS_IN) for a in mid2]

    def run(blocks):
        total = None
        for c in range(CHUNKS):
            total = project(blocks(c), weights, c, total)
        return total, swap(total)

    first = run(lambda c: [(own[c],), (near[c],)])
    second = run(lambda c: [(mid[c], end2[c])])
    third = run(lambda c: [(mid2[c], end3[c])])

    slots = [rows, rows, rows, rows]
    columns = w_out.shape[1] // CHUNKS
    attended, mixed = attend_out([first, second, third], w_out, kv_width, slots, columns)
    result = []
    for c in range(CHUNKS):
        if c > 0:
            mixed = out_again(attended, w_out, slots, c, columns)
        m_own, m_near, m_second, m_third = mixed
        r1 = hop(m_third, ENDS_OUT)
        r2e = hop(m_second, ENDS_OUT)
        r2m = hop(m_third + r1, MIDDLE)
        r3m = hop(m_second + r2e, MIDDLE)
        r3x = hop(m_near + r2m, PAIRS)
        result.append(m_own + (r3x + r3m))
    return jnp.concatenate(result, axis=1)


def on_device(tokens, w_query, w_key, w_value, w_out):
    highest = lax.Precision.HIGHEST
    gathered = lax.all_gather(tokens, "col", axis=0, tiled=True)
    q_width = w_query.shape[1]
    kv_width = w_key.shape[1]

    def product(weight):
        return jnp.dot(gathered, weight, preferred_element_type=jnp.float32, precision=highest)

    joined = lax.psum_scatter(
        jnp.concatenate([product(w_query), product(w_key), product(w_value)], axis=1),
        "row",
        scatter_dimension=0,
        tiled=True,
    )
    query_rows = joined[:, :q_width]
    keys = lax.all_gather(joined[:, q_width : q_width + kv_width], "row", axis=0, tiled=True)
    values = lax.all_gather(joined[:, q_width + kv_width :], "row", axis=0, tiled=True)
    count_of_rows, count_of_heads = query_rows.shape[0], kv_width // HEAD_SIZE_DIM
    query_rows = query_rows.reshape(count_of_rows, count_of_heads, GROUP, HEAD_SIZE_DIM)
    keys = keys.reshape(-1, count_of_heads, HEAD_SIZE_DIM)
    values = values.reshape(-1, count_of_heads, HEAD_SIZE_DIM)
    scores = jnp.einsum("rkgd,nkd->kgrn", query_rows, keys, precision=highest)
    weights = jax.nn.softmax(scores * (1.0 / math.sqrt(HEAD_SIZE_DIM)), axis=-1)
    attended = jnp.einsum("kgrn,nkd->rkgd", weights, values, precision=highest)
    attended = lax.all_gather(attended.reshape(count_of_rows, q_width), "row", axis=0, tiled=True)
    return lax.psum_scatter(
        jnp.dot(attended, w_out, preferred_element_type=jnp.float32, precision=highest),
        "col",
        scatter_dimension=0,
        tiled=True,
    )


def solution(mesh):
    placed = (
        P(("depth", "col"), "row"),
        P("row", "col"),
        P("row", "col"),
        P("row", "col"),
        P("col", "row"),
    )
    here = mesh.shape["row"] == 2 and mesh.shape["col"] == 4
    return jax.shard_map(
        on_line_of_four if here else on_device,
        mesh=mesh,
        in_specs=placed,
        out_specs=P(("depth", "col"), "row"),
        check_vma=False,
    )
```

```python
import functools
import math

import jax
import jax.numpy as jnp
from jax import lax
from jax.experimental import pallas as pl
from jax.experimental.pallas import tpu as pltpu
from jax.sharding import PartitionSpec as P

QUERY_HEADS = 32
KEY_VALUE_HEADS = 4
HEAD_SIZE_DIM = 128
GROUP = QUERY_HEADS // KEY_VALUE_HEADS

VMEM_LIMIT = 40 * 1024 * 1024

ENDS_IN = [(1, 0), (2, 3)]
ENDS_OUT = [(0, 1), (3, 2)]
PAIRS = [(0, 1), (1, 0), (2, 3), (3, 2)]
MIDDLE = [(1, 2), (2, 1)]
CORES = [(0, 1), (1, 0)]


def split(a):
    high = a.astype(jnp.bfloat16)
    return high, (a - high.astype(jnp.float32)).astype(jnp.bfloat16)


def dot(a, b, dims=((1,), (0,))):
    return lax.dot_general(a, b, (dims, ((), ())), preferred_element_type=jnp.float32)


def dot3(a, b, dims=((1,), (0,))):
    rows = a[0].shape[0]
    both = dot(jnp.concatenate(a, axis=0), b[0], dims)
    return both[:rows] + (both[rows:] + dot(a[0], b[1], dims))


def project_kernel(terms, with_total, *refs):
    n_x = sum(terms)
    x_refs, (wq, wk, wv), rest = refs[:n_x], refs[n_x : n_x + 3], refs[n_x + 3 :]
    out = rest[-1]

    @pl.when(pl.program_id(0) == 0)
    def _():
        out[...] = rest[0][...] if with_total else jnp.zeros_like(out)

    blocks, at = [], 0
    for n in terms:
        block = x_refs[at][...]
        for r in x_refs[at + 1 : at + n]:
            block = block + r[...]
        blocks.append(block)
        at += n
    x = split(jnp.concatenate(blocks, axis=0) if len(blocks) > 1 else blocks[0])
    offset = 0
    for w in (wq, wk, wv):
        width = w.shape[1]
        out[:, offset : offset + width] += dot3(x, split(w[...]))
        offset += width


def project(blocks, weights, chunk, total=None, step=512):
    terms = tuple(len(b) for b in blocks)
    flat = [a for b in blocks for a in b]
    depth = flat[0].shape[1]
    rows = sum(b[0].shape[0] for b in blocks)
    steps = depth // step
    width = sum(w.shape[1] for w in weights)
    first = chunk * steps
    in_specs = [pl.BlockSpec((a.shape[0], step), lambda k: (0, k)) for a in flat]
    in_specs += [pl.BlockSpec((step, w.shape[1]), lambda k: (first + k, 0)) for w in weights]
    operands = flat + list(weights)
    if total is not None:
        in_specs.append(pl.BlockSpec((rows, width), lambda k: (0, 0)))
        operands.append(total)
    return pl.pallas_call(
        functools.partial(project_kernel, terms, total is not None),
        grid=(steps,),
        in_specs=in_specs,
        out_specs=pl.BlockSpec((rows, width), lambda k: (0, 0)),
        out_shape=jax.ShapeDtypeStruct((rows, width), jnp.float32),
        compiler_params=pltpu.CompilerParams(vmem_limit_bytes=VMEM_LIMIT),
        cost_estimate=pl.CostEstimate(
            flops=6 * rows * depth * width, bytes_accessed=4 * depth * (rows + width), transcendentals=0
        ),
        name="project",
    )(*operands)


def attend(keyed, asked, q_width, kv_width, store):
    groups = kv_width // HEAD_SIZE_DIM
    scale = 1.0 / math.sqrt(HEAD_SIZE_DIM)

    def columns(pairs, start):
        stop = start + HEAD_SIZE_DIM
        return jnp.concatenate([a[:, start:stop] + b[:, start:stop] for a, b in pairs], axis=0)

    rows = sum(a.shape[0] for a, _ in asked)
    together = GROUP if rows <= 64 else 1
    for g in range(groups):
        at = q_width + g * HEAD_SIZE_DIM
        k_high, k_low = split(columns(keyed, at))
        v_high, v_low = split(columns(keyed, at + kv_width))
        k_both = jnp.concatenate([k_high, k_high], axis=1)
        v_both = jnp.concatenate([v_high, v_low], axis=1)
        for j in range(0, GROUP, together):
            heads = [(g * GROUP + j + i) * HEAD_SIZE_DIM for i in range(together)]
            q_high, q_low = split(jnp.concatenate([columns(asked, h) for h in heads], axis=0) * scale)
            scores = dot(jnp.concatenate([q_high, q_low], axis=1), k_both, ((1,), (1,)))
            scores = scores + dot(q_high, k_low, ((1,), (1,)))
            weights = jnp.exp(scores - jnp.max(scores, axis=-1, keepdims=True))
            total = jnp.sum(weights, axis=-1, keepdims=True)
            p_high, p_low = split(weights)
            both = dot(p_high, v_both)
            result = both[:, :HEAD_SIZE_DIM] + (both[:, HEAD_SIZE_DIM:] + dot(p_low, v_high))
            result = result / total
            for i, h in enumerate(heads):
                store(h, result[i * rows : (i + 1) * rows])


def mix(high, low, w_ref, outs):
    mixed = dot3((high[...], low[...]), split(w_ref[...]))
    at = 0
    for o in outs:
        o[...] = mixed[at : at + o.shape[0]]
        at += o.shape[0]


def attend_out_kernel(n_parts, first, last, q_width, kv_width, *refs):
    part_refs, w_ref, rest = refs[: 2 * n_parts], refs[2 * n_parts], refs[2 * n_parts + 1 :]
    high, low, outs = rest[0], rest[1], rest[2:]

    @pl.when(pl.program_id(0) == 0)
    def _():
        def store(head, rows):
            h, l = split(rows)
            high[:, head : head + HEAD_SIZE_DIM] = h
            low[:, head : head + HEAD_SIZE_DIM] = l

        pairs = [(part_refs[2 * i], part_refs[2 * i + 1]) for i in range(n_parts)]
        attend(pairs, pairs[first:last], q_width, kv_width, store)

    mix(high, low, w_ref, outs)


def mix_kernel(high, low, w_ref, *outs):
    mix(high, low, w_ref, outs)


def attend_out(parts, first, last, w_out, kv_width, slots, columns, step=512):
    rows = sum(a.shape[0] for a, _ in parts[first:last])
    keyed = sum(a.shape[0] for a, _ in parts)
    q_width = w_out.shape[0]
    flat = [r for pair in parts for r in pair]
    whole = pl.BlockSpec((rows, q_width), lambda n: (0, 0))
    bf16 = jax.ShapeDtypeStruct((rows, q_width), jnp.bfloat16)
    res = pl.pallas_call(
        functools.partial(attend_out_kernel, len(parts), first, last, q_width, kv_width),
        grid=(columns // step,),
        in_specs=[pl.BlockSpec(a.shape, lambda n: (0, 0)) for a in flat]
        + [pl.BlockSpec((q_width, step), lambda n: (0, n))],
        out_specs=[whole, whole] + [pl.BlockSpec((s, step), lambda n: (0, n)) for s in slots],
        out_shape=[bf16, bf16] + [jax.ShapeDtypeStruct((s, columns), jnp.float32) for s in slots],
        compiler_params=pltpu.CompilerParams(vmem_limit_bytes=VMEM_LIMIT),
        cost_estimate=pl.CostEstimate(
            flops=6 * rows * q_width * columns + 24 * rows * keyed * q_width,
            bytes_accessed=4 * columns * (q_width + rows),
            transcendentals=rows * keyed * q_width // HEAD_SIZE_DIM,
        ),
        name="attend_out",
    )(*flat, w_out)
    return res[:2], res[2:]


def out_again(attended, w_out, slots, start, columns, step=512):
    high, low = attended
    rows, q_width = high.shape
    first = start // step
    whole = pl.BlockSpec((rows, q_width), lambda n: (0, 0))
    return pl.pallas_call(
        mix_kernel,
        grid=(columns // step,),
        in_specs=[whole, whole, pl.BlockSpec((q_width, step), lambda n: (0, first + n))],
        out_specs=[pl.BlockSpec((s, step), lambda n: (0, n)) for s in slots],
        out_shape=[jax.ShapeDtypeStruct((s, columns), jnp.float32) for s in slots],
        compiler_params=pltpu.CompilerParams(vmem_limit_bytes=VMEM_LIMIT),
        cost_estimate=pl.CostEstimate(
            flops=6 * rows * q_width * columns, bytes_accessed=4 * columns * (q_width + rows), transcendentals=0
        ),
        name="out_again",
    )(high, low, w_out)


def after(a, *others):
    return lax.optimization_barrier((a, *others))[0]


CHUNKS = 2


def on_line_of_four(tokens, w_query, w_key, w_value, w_out):
    rows, depth = tokens.shape
    weights = (w_query, w_key, w_value)
    kv_width = w_key.shape[1]
    step = depth // CHUNKS

    def hop(a, pairs):
        return lax.ppermute(a, "col", pairs)

    def swap(a):
        return lax.ppermute(a, "row", CORES)

    def run(blocks, total=None):
        for c in range(CHUNKS):
            total = project(blocks(c), weights, c, total)
        return total

    own = [tokens[:, c * step : (c + 1) * step] for c in range(CHUNKS)]
    near = [hop(a, PAIRS) for a in own]
    mid = [hop(a, MIDDLE) for a in own]
    end2 = [hop(a, ENDS_IN) for a in mid]
    mid2 = [hop(a, MIDDLE) for a in near]
    first = run(lambda c: [(own[c],), (near[c],)])
    mid2 = [after(a, first) for a in mid2]
    first = (first, swap(first))
    end3 = [hop(a, ENDS_IN) for a in mid2]
    second = run(lambda c: [(mid[c], end2[c])])
    second = (second, swap(second))
    third = run(lambda c: [(mid2[c], end3[c])])
    third = (third, swap(third))

    columns = w_out.shape[1] // CHUNKS
    parts = [first, second, third]
    a_third, m_third = attend_out(parts, 2, 3, w_out, kv_width, [rows], columns)
    m_third = [m_third[0]] + [
        out_again(a_third, w_out, [rows], c * columns, columns)[0] for c in range(1, CHUNKS)
    ]
    r1 = [hop(m, ENDS_OUT) for m in m_third]
    others = [tuple(after(a, *m_third) for a in first), second, third]
    a_rest, mixed = attend_out(others, 0, 2, w_out, kv_width, [rows] * 3, columns)
    result = []
    for c in range(CHUNKS):
        if c > 0:
            mixed = out_again(a_rest, w_out, [rows] * 3, c * columns, columns)
        m_own, m_near, m_second = mixed
        r2e = hop(m_second, ENDS_OUT)
        r2m = hop(m_third[c] + r1[c], MIDDLE)
        r3m = hop(m_second + r2e, MIDDLE)
        r3x = hop(m_near + r2m, PAIRS)
        result.append(m_own + (r3x + r3m))
    return jnp.concatenate(result, axis=1)


def on_device(tokens, w_query, w_key, w_value, w_out):
    highest = lax.Precision.HIGHEST
    gathered = lax.all_gather(tokens, "col", axis=0, tiled=True)
    q_width = w_query.shape[1]
    kv_width = w_key.shape[1]

    def product(weight):
        return jnp.dot(gathered, weight, preferred_element_type=jnp.float32, precision=highest)

    joined = lax.psum_scatter(
        jnp.concatenate([product(w_query), product(w_key), product(w_value)], axis=1),
        "row",
        scatter_dimension=0,
        tiled=True,
    )
    query_rows = joined[:, :q_width]
    keys = lax.all_gather(joined[:, q_width : q_width + kv_width], "row", axis=0, tiled=True)
    values = lax.all_gather(joined[:, q_width + kv_width :], "row", axis=0, tiled=True)
    count_of_rows, count_of_heads = query_rows.shape[0], kv_width // HEAD_SIZE_DIM
    query_rows = query_rows.reshape(count_of_rows, count_of_heads, GROUP, HEAD_SIZE_DIM)
    keys = keys.reshape(-1, count_of_heads, HEAD_SIZE_DIM)
    values = values.reshape(-1, count_of_heads, HEAD_SIZE_DIM)
    scores = jnp.einsum("rkgd,nkd->kgrn", query_rows, keys, precision=highest)
    weights = jax.nn.softmax(scores * (1.0 / math.sqrt(HEAD_SIZE_DIM)), axis=-1)
    attended = jnp.einsum("kgrn,nkd->rkgd", weights, values, precision=highest)
    attended = lax.all_gather(attended.reshape(count_of_rows, q_width), "row", axis=0, tiled=True)
    return lax.psum_scatter(
        jnp.dot(attended, w_out, preferred_element_type=jnp.float32, precision=highest),
        "col",
        scatter_dimension=0,
        tiled=True,
    )


def solution(mesh):
    placed = (
        P(("depth", "col"), "row"),
        P("row", "col"),
        P("row", "col"),
        P("row", "col"),
        P("col", "row"),
    )
    here = mesh.shape["row"] == 2 and mesh.shape["col"] == 4
    return jax.shard_map(
        on_line_of_four if here else on_device,
        mesh=mesh,
        in_specs=placed,
        out_specs=P(("depth", "col"), "row"),
        check_vma=False,
    )
```

```python
import functools
import math

import jax
import jax.numpy as jnp
from jax import lax
from jax.experimental import pallas as pl
from jax.experimental.pallas import tpu as pltpu
from jax.sharding import PartitionSpec as P

QUERY_HEADS = 32
KEY_VALUE_HEADS = 4
HEAD_SIZE_DIM = 128
GROUP = QUERY_HEADS // KEY_VALUE_HEADS

VMEM_LIMIT = 40 * 1024 * 1024

ENDS_IN = [(1, 0), (2, 3)]
ENDS_OUT = [(0, 1), (3, 2)]
PAIRS = [(0, 1), (1, 0), (2, 3), (3, 2)]
MIDDLE = [(1, 2), (2, 1)]
CORES = [(0, 1), (1, 0)]

OUT_EIGHTHS = (4, 4)


def split(a):
    high = a.astype(jnp.bfloat16)
    return high, (a - high.astype(jnp.float32)).astype(jnp.bfloat16)


def dot(a, b, dims=((1,), (0,))):
    return lax.dot_general(a, b, (dims, ((), ())), preferred_element_type=jnp.float32)


def dot3(a, b, dims=((1,), (0,))):
    rows = a[0].shape[0]
    both = dot(jnp.concatenate(a, axis=0), b[0], dims)
    return both[:rows] + (both[rows:] + dot(a[0], b[1], dims))


def project_kernel(terms, with_total, *refs):
    n_x = sum(terms)
    x_refs, (wq, wk, wv), rest = refs[:n_x], refs[n_x : n_x + 3], refs[n_x + 3 :]
    out = rest[-1]

    @pl.when(pl.program_id(0) == 0)
    def _():
        out[...] = rest[0][...] if with_total else jnp.zeros_like(out)

    blocks, at = [], 0
    for n in terms:
        block = x_refs[at][...]
        for r in x_refs[at + 1 : at + n]:
            block = block + r[...]
        blocks.append(block)
        at += n
    x = split(jnp.concatenate(blocks, axis=0) if len(blocks) > 1 else blocks[0])
    offset = 0
    for w in (wq, wk, wv):
        width = w.shape[1]
        out[:, offset : offset + width] += dot3(x, split(w[...]))
        offset += width


def project(blocks, weights, start, depth, total=None, step=512):
    terms = tuple(len(b) for b in blocks)
    flat = [t for b in blocks for t in b]
    rows = sum(b[0][0].shape[0] for b in blocks)
    width = sum(w.shape[1] for w in weights)
    first = start // step

    def columns(a, at):
        return pl.BlockSpec((a.shape[0], step), lambda k: (0, at // step + k))

    in_specs = [columns(a, at) for a, at in flat]
    in_specs += [pl.BlockSpec((step, w.shape[1]), lambda k: (first + k, 0)) for w in weights]
    operands = [a for a, _ in flat] + list(weights)
    if total is not None:
        in_specs.append(pl.BlockSpec((rows, width), lambda k: (0, 0)))
        operands.append(total)
    return pl.pallas_call(
        functools.partial(project_kernel, terms, total is not None),
        grid=(depth // step,),
        in_specs=in_specs,
        out_specs=pl.BlockSpec((rows, width), lambda k: (0, 0)),
        out_shape=jax.ShapeDtypeStruct((rows, width), jnp.float32),
        compiler_params=pltpu.CompilerParams(vmem_limit_bytes=VMEM_LIMIT),
        cost_estimate=pl.CostEstimate(
            flops=6 * rows * depth * width, bytes_accessed=4 * depth * (rows + width), transcendentals=0
        ),
        name="project",
    )(*operands)


def attend(keyed, asked, q_width, kv_width, store):
    groups = kv_width // HEAD_SIZE_DIM
    scale = 1.0 / math.sqrt(HEAD_SIZE_DIM)

    def columns(pairs, start):
        stop = start + HEAD_SIZE_DIM
        return jnp.concatenate([a[:, start:stop] + b[:, start:stop] for a, b in pairs], axis=0)

    rows = sum(a.shape[0] for a, _ in asked)
    together = GROUP if rows <= 64 else 1
    for g in range(groups):
        at = q_width + g * HEAD_SIZE_DIM
        k_high, k_low = split(columns(keyed, at))
        v_high, v_low = split(columns(keyed, at + kv_width))
        k_both = jnp.concatenate([k_high, k_high], axis=1)
        v_both = jnp.concatenate([v_high, v_low], axis=1)
        for j in range(0, GROUP, together):
            heads = [(g * GROUP + j + i) * HEAD_SIZE_DIM for i in range(together)]
            q_high, q_low = split(jnp.concatenate([columns(asked, h) for h in heads], axis=0) * scale)
            scores = dot(jnp.concatenate([q_high, q_low], axis=1), k_both, ((1,), (1,)))
            scores = scores + dot(q_high, k_low, ((1,), (1,)))
            weights = jnp.exp(scores - jnp.max(scores, axis=-1, keepdims=True))
            total = jnp.sum(weights, axis=-1, keepdims=True)
            p_high, p_low = split(weights)
            both = dot(p_high, v_both)
            result = both[:, :HEAD_SIZE_DIM] + (both[:, HEAD_SIZE_DIM:] + dot(p_low, v_high))
            result = result / total
            for i, h in enumerate(heads):
                store(h, result[i * rows : (i + 1) * rows])


def mix(high, low, w_ref, outs):
    mixed = dot3((high[...], low[...]), split(w_ref[...]))
    at = 0
    for o in outs:
        o[...] = mixed[at : at + o.shape[0]]
        at += o.shape[0]


def attend_out_kernel(n_parts, first, last, q_width, kv_width, *refs):
    part_refs, w_ref, rest = refs[: 2 * n_parts], refs[2 * n_parts], refs[2 * n_parts + 1 :]
    high, low, outs = rest[0], rest[1], rest[2:]

    @pl.when(pl.program_id(0) == 0)
    def _():
        def store(head, rows):
            h, l = split(rows)
            high[:, head : head + HEAD_SIZE_DIM] = h
            low[:, head : head + HEAD_SIZE_DIM] = l

        pairs = [(part_refs[2 * i], part_refs[2 * i + 1]) for i in range(n_parts)]
        attend(pairs, pairs[first:last], q_width, kv_width, store)

    mix(high, low, w_ref, outs)


def mix_kernel(high, low, w_ref, *outs):
    mix(high, low, w_ref, outs)


def attend_out(parts, first, last, w_out, kv_width, slots, columns, step=512):
    rows = sum(a.shape[0] for a, _ in parts[first:last])
    keyed = sum(a.shape[0] for a, _ in parts)
    q_width = w_out.shape[0]
    flat = [r for pair in parts for r in pair]
    whole = pl.BlockSpec((rows, q_width), lambda n: (0, 0))
    bf16 = jax.ShapeDtypeStruct((rows, q_width), jnp.bfloat16)
    res = pl.pallas_call(
        functools.partial(attend_out_kernel, len(parts), first, last, q_width, kv_width),
        grid=(columns // step,),
        in_specs=[pl.BlockSpec(a.shape, lambda n: (0, 0)) for a in flat]
        + [pl.BlockSpec((q_width, step), lambda n: (0, n))],
        out_specs=[whole, whole] + [pl.BlockSpec((s, step), lambda n: (0, n)) for s in slots],
        out_shape=[bf16, bf16] + [jax.ShapeDtypeStruct((s, columns), jnp.float32) for s in slots],
        compiler_params=pltpu.CompilerParams(vmem_limit_bytes=VMEM_LIMIT),
        cost_estimate=pl.CostEstimate(
            flops=6 * rows * q_width * columns + 24 * rows * keyed * q_width,
            bytes_accessed=4 * columns * (q_width + rows),
            transcendentals=rows * keyed * q_width // HEAD_SIZE_DIM,
        ),
        name="attend_out",
    )(*flat, w_out)
    return res[:2], res[2:]


def out_again(attended, w_out, slots, start, columns, step=512):
    high, low = attended
    rows, q_width = high.shape
    first = start // step
    whole = pl.BlockSpec((rows, q_width), lambda n: (0, 0))
    return pl.pallas_call(
        mix_kernel,
        grid=(columns // step,),
        in_specs=[whole, whole, pl.BlockSpec((q_width, step), lambda n: (0, first + n))],
        out_specs=[pl.BlockSpec((s, step), lambda n: (0, n)) for s in slots],
        out_shape=[jax.ShapeDtypeStruct((s, columns), jnp.float32) for s in slots],
        compiler_params=pltpu.CompilerParams(vmem_limit_bytes=VMEM_LIMIT),
        cost_estimate=pl.CostEstimate(
            flops=6 * rows * q_width * columns, bytes_accessed=4 * columns * (q_width + rows), transcendentals=0
        ),
        name="out_again",
    )(high, low, w_out)


def after(a, *others):
    return lax.optimization_barrier((a, *others))[0]


def cut(sizes):
    return [(sum(sizes[:i]), size) for i, size in enumerate(sizes)]


def on_line_of_four(tokens, w_query, w_key, w_value, w_out):
    rows, depth = tokens.shape
    weights = (w_query, w_key, w_value)
    kv_width = w_key.shape[1]
    halves = cut([depth // 2] * 2)
    last = cut([depth // 2, depth // 4, depth // 4])

    def hop(a, pairs):
        return lax.ppermute(a, "col", pairs)

    def swap(a):
        return lax.ppermute(a, "row", CORES)

    def columns(a, start, size):
        return a[:, start : start + size]

    own = [columns(tokens, *h) for h in halves]
    near = [hop(a, PAIRS) for a in own]
    mid = [hop(a, MIDDLE) for a in own]
    mid2 = [hop(a, MIDDLE) for a in near]
    end2 = [hop(a, ENDS_IN) for a in mid]
    first = second = third = None
    for h, o, n in zip(halves, own, near):
        first = project([((o, 0),), ((n, 0),)], weights, *h, first)
    mid2[0] = after(mid2[0], first)
    second = project([((mid[0], 0), (end2[0], 0))], weights, *halves[0])
    mid2[1] = after(mid2[1], second)
    second = project([((mid[1], 0), (end2[1], 0))], weights, *halves[1], second)
    first, second = [(a, swap(a)) for a in (first, second)]
    for start, size in last:
        half = start // halves[0][1]
        at = start - halves[half][0]
        end3 = hop(columns(mid2[half], at, size) if size < halves[0][1] else mid2[half], ENDS_IN)
        third = project([((mid2[half], at), (end3, 0))], weights, start, size, third)
    third = (third, swap(third))

    width = w_out.shape[1]
    pieces = cut([width // 8 * n for n in OUT_EIGHTHS])
    parts = [first, second, third]
    a_third, m_third = attend_out(parts, 2, 3, w_out, kv_width, [rows], pieces[0][1])
    m_third = list(m_third) + [out_again(a_third, w_out, [rows], *p)[0] for p in pieces[1:]]
    r1 = [hop(m, ENDS_OUT) for m in m_third]
    others = [tuple(after(a, *m_third) for a in first), second, third]
    a_rest, mixed = attend_out(others, 0, 2, w_out, kv_width, [rows] * 3, pieces[0][1])
    result = []
    for c, piece in enumerate(pieces):
        if c > 0:
            mixed = out_again(a_rest, w_out, [rows] * 3, *piece)
        m_own, m_near, m_second = mixed
        r2e = hop(m_second, ENDS_OUT)
        r2m = hop(m_third[c] + r1[c], MIDDLE)
        r3m = hop(m_second + r2e, MIDDLE)
        r3x = hop(m_near + r2m, PAIRS)
        result.append(m_own + (r3x + r3m))
    return jnp.concatenate(result, axis=1)


def on_device(tokens, w_query, w_key, w_value, w_out):
    highest = lax.Precision.HIGHEST
    gathered = lax.all_gather(tokens, "col", axis=0, tiled=True)
    q_width = w_query.shape[1]
    kv_width = w_key.shape[1]

    def product(weight):
        return jnp.dot(gathered, weight, preferred_element_type=jnp.float32, precision=highest)

    joined = lax.psum_scatter(
        jnp.concatenate([product(w_query), product(w_key), product(w_value)], axis=1),
        "row",
        scatter_dimension=0,
        tiled=True,
    )
    query_rows = joined[:, :q_width]
    keys = lax.all_gather(joined[:, q_width : q_width + kv_width], "row", axis=0, tiled=True)
    values = lax.all_gather(joined[:, q_width + kv_width :], "row", axis=0, tiled=True)
    count_of_rows, count_of_heads = query_rows.shape[0], kv_width // HEAD_SIZE_DIM
    query_rows = query_rows.reshape(count_of_rows, count_of_heads, GROUP, HEAD_SIZE_DIM)
    keys = keys.reshape(-1, count_of_heads, HEAD_SIZE_DIM)
    values = values.reshape(-1, count_of_heads, HEAD_SIZE_DIM)
    scores = jnp.einsum("rkgd,nkd->kgrn", query_rows, keys, precision=highest)
    weights = jax.nn.softmax(scores * (1.0 / math.sqrt(HEAD_SIZE_DIM)), axis=-1)
    attended = jnp.einsum("kgrn,nkd->rkgd", weights, values, precision=highest)
    attended = lax.all_gather(attended.reshape(count_of_rows, q_width), "row", axis=0, tiled=True)
    return lax.psum_scatter(
        jnp.dot(attended, w_out, preferred_element_type=jnp.float32, precision=highest),
        "col",
        scatter_dimension=0,
        tiled=True,
    )


def solution(mesh):
    placed = (
        P(("depth", "col"), "row"),
        P("row", "col"),
        P("row", "col"),
        P("row", "col"),
        P("col", "row"),
    )
    here = mesh.shape["row"] == 2 and mesh.shape["col"] == 4
    return jax.shard_map(
        on_line_of_four if here else on_device,
        mesh=mesh,
        in_specs=placed,
        out_specs=P(("depth", "col"), "row"),
        check_vma=False,
    )
```

```python
import functools
import math

import jax
import jax.numpy as jnp
from jax import lax
from jax.experimental import pallas as pl
from jax.experimental.pallas import tpu as pltpu
from jax.sharding import PartitionSpec as P

QUERY_HEADS = 32
KEY_VALUE_HEADS = 4
HEAD_SIZE_DIM = 128
GROUP = QUERY_HEADS // KEY_VALUE_HEADS

VMEM_LIMIT = 38 * 1024 * 1024

ENDS_IN = [(1, 0), (2, 3)]
ENDS_OUT = [(0, 1), (3, 2)]
PAIRS = [(0, 1), (1, 0), (2, 3), (3, 2)]
MIDDLE = [(1, 2), (2, 1)]
CORES = [(0, 1), (1, 0)]


def split(a):
    high = a.astype(jnp.bfloat16)
    return high, (a - high.astype(jnp.float32)).astype(jnp.bfloat16)


def dot(a, b, dims=((1,), (0,))):
    return lax.dot_general(a, b, (dims, ((), ())), preferred_element_type=jnp.float32)


def dot3(a, b, dims=((1,), (0,))):
    rows = a[0].shape[0]
    both = dot(jnp.concatenate(a, axis=0), b[0], dims)
    return both[:rows] + (both[rows:] + dot(a[0], b[1], dims))


def project_kernel(terms, with_total, first, steps, step, n_before, *refs):
    n_x = sum(len(t) for t in terms)
    x_refs, w_refs, rest = refs[:n_x], refs[n_x : n_x + 3], refs[n_x + 3 :]
    total, rest = rest[0], rest[(1 if with_total else 0) + n_before :]
    out, kept, bufs, sems = rest[0], rest[1:-4], rest[-4:-1], rest[-1]

    def copies(k):
        rows = pl.ds(first + k * step, step)
        return [pltpu.make_async_copy(w.at[rows], b.at[k], sems.at[k, i]) for i, (w, b) in enumerate(zip(w_refs, bufs))]

    for k in range(bufs[0].shape[0]):
        for c in copies(k):
            c.start()
    for k in range(steps):
        blocks, i = [], 0
        for term in terms:
            block = None
            for at in term:
                piece = x_refs[i][:, at + k * step : at + (k + 1) * step]
                block = piece if block is None else block + piece
                i += 1
            blocks.append(block)
        x = split(jnp.concatenate(blocks, axis=0) if len(blocks) > 1 else blocks[0])
        for c in copies(k):
            c.wait()
        offset = 0
        for b in bufs:
            width = b.shape[2]
            columns = slice(offset, offset + width)
            product = dot3(x, split(b[k]))
            if k > 0:
                out[:, columns] += product
            elif with_total:
                out[:, columns] = total[:, columns] + product
            else:
                out[:, columns] = product
            offset += width
    for k in range(steps, bufs[0].shape[0]):
        for c in copies(k):
            c.wait()
        offset, rows = 0, slice((k - steps) * step, (k - steps + 1) * step)
        for b in bufs:
            columns = slice(offset, offset + b.shape[2])
            kept[0][rows, columns], kept[1][rows, columns] = split(b[k])
            offset += b.shape[2]


def project(blocks, weights, start, depth, total=None, keep=0, before=(), step=512):
    terms = tuple(tuple(at for _, at in b) for b in blocks)
    operands = [a for b in blocks for a, _ in b]
    rows = sum(b[0][0].shape[0] for b in blocks)
    width = sum(w.shape[1] for w in weights)
    steps = depth // step
    vmem, anywhere = pl.BlockSpec(memory_space=pltpu.VMEM), pl.BlockSpec(memory_space=pl.ANY)
    in_specs = [vmem] * len(operands) + [anywhere] * len(weights)
    operands += weights
    if total is not None:
        in_specs.append(vmem)
        operands.append(total)
    in_specs += [anywhere] * len(before)
    operands += before
    return pl.pallas_call(
        functools.partial(project_kernel, terms, total is not None, start, steps, step, len(before)),
        in_specs=in_specs,
        out_specs=[vmem] * 3 if keep else vmem,
        out_shape=[jax.ShapeDtypeStruct((rows, width), jnp.float32)]
        + [jax.ShapeDtypeStruct((keep, width), jnp.bfloat16)] * 2
        if keep
        else jax.ShapeDtypeStruct((rows, width), jnp.float32),
        scratch_shapes=[pltpu.VMEM((steps + keep // step, step, w.shape[1]), jnp.float32) for w in weights]
        + [pltpu.SemaphoreType.DMA((steps + keep // step, len(weights)))],
        compiler_params=pltpu.CompilerParams(vmem_limit_bytes=VMEM_LIMIT),
        cost_estimate=pl.CostEstimate(
            flops=6 * rows * depth * width, bytes_accessed=4 * depth * (rows + width), transcendentals=0
        ),
        name="project",
    )(*operands)


def project_last_kernel(at, x, y, high, low, total, out):
    size = y.shape[1]
    block = split(x[:, at : at + size] + y[...])
    out[...] = total[...] + dot3(block, (high[...], low[...]))


def project_last(block, kept, total):
    (x, at), (y, _) = block
    vmem = pl.BlockSpec(memory_space=pltpu.VMEM)
    return pl.pallas_call(
        functools.partial(project_last_kernel, at),
        in_specs=[vmem] * 5,
        out_specs=vmem,
        out_shape=jax.ShapeDtypeStruct(total.shape, jnp.float32),
        compiler_params=pltpu.CompilerParams(vmem_limit_bytes=VMEM_LIMIT),
        cost_estimate=pl.CostEstimate(
            flops=6 * y.shape[1] * total.size, bytes_accessed=4 * y.shape[1] * total.shape[1], transcendentals=0
        ),
        name="project_last",
    )(x, y, *kept, total)


def attend(keyed, asked, q_width, kv_width, store):
    groups = kv_width // HEAD_SIZE_DIM
    scale = 1.0 / math.sqrt(HEAD_SIZE_DIM)

    def columns(pairs, start):
        stop = start + HEAD_SIZE_DIM
        return jnp.concatenate([a[:, start:stop] + b[:, start:stop] for a, b in pairs], axis=0)

    rows = sum(a.shape[0] for a, _ in asked)
    together = GROUP if rows <= 64 else 1
    for g in range(groups):
        at = q_width + g * HEAD_SIZE_DIM
        k_high, k_low = split(columns(keyed, at))
        v_high, v_low = split(columns(keyed, at + kv_width))
        k_both = jnp.concatenate([k_high, k_high], axis=1)
        v_both = jnp.concatenate([v_high, v_low], axis=1)
        for j in range(0, GROUP, together):
            heads = [(g * GROUP + j + i) * HEAD_SIZE_DIM for i in range(together)]
            q_high, q_low = split(jnp.concatenate([columns(asked, h) for h in heads], axis=0) * scale)
            scores = dot(jnp.concatenate([q_high, q_low], axis=1), k_both, ((1,), (1,)))
            scores = scores + dot(q_high, k_low, ((1,), (1,)))
            weights = jnp.exp(scores - jnp.max(scores, axis=-1, keepdims=True))
            total = jnp.sum(weights, axis=-1, keepdims=True)
            p_high, p_low = split(weights)
            both = dot(p_high, v_both)
            result = both[:, :HEAD_SIZE_DIM] + (both[:, HEAD_SIZE_DIM:] + dot(p_low, v_high))
            result = result / total
            for i, h in enumerate(heads):
                store(h, result[i * rows : (i + 1) * rows])


def halve_kernel(start, w_ref, before, high, low, buf, sems):
    steps, step, size = buf.shape

    def copy(k):
        return pltpu.make_async_copy(w_ref.at[pl.ds(k * step, step), pl.ds(start, size)], buf.at[k], sems.at[k])

    for k in range(steps):
        copy(k).start()
    for k in range(steps):
        copy(k).wait()
        rows = slice(k * step, (k + 1) * step)
        high[rows], low[rows] = split(buf[k])


def halve(w, start, size, before, step=256):
    steps = w.shape[0] // step
    vmem, anywhere = pl.BlockSpec(memory_space=pltpu.VMEM), pl.BlockSpec(memory_space=pl.ANY)
    return pl.pallas_call(
        functools.partial(halve_kernel, start),
        in_specs=[anywhere] * 2,
        out_specs=[vmem] * 2,
        out_shape=[jax.ShapeDtypeStruct((w.shape[0], size), jnp.bfloat16)] * 2,
        scratch_shapes=[pltpu.VMEM((steps, step, size), jnp.float32), pltpu.SemaphoreType.DMA((steps,))],
        compiler_params=pltpu.CompilerParams(vmem_limit_bytes=VMEM_LIMIT),
        cost_estimate=pl.CostEstimate(flops=w.shape[0] * size, bytes_accessed=8 * w.shape[0] * size, transcendentals=0),
        name="halve",
    )(w, before)


def mix_kernel(n_parts, ask, q_width, kv_width, start, step, *refs):
    part_refs, rest = refs[:n_parts], refs[n_parts:]
    if start is None:
        (w_high, w_low), outs = rest[:2], rest[2:]
    else:
        w_ref, outs, (buf, sems) = rest[0], rest[1:-2], rest[-2:]

        def copy(k):
            return pltpu.make_async_copy(w_ref.at[:, pl.ds(start + k * step, step)], buf.at[k], sems.at[k])

        for k in range(buf.shape[0]):
            copy(k).start()
    if ask is None:
        high, low = part_refs
    else:
        high, low, outs = outs[0], outs[1], outs[2:]

        def store(head, rows):
            h, l = split(rows)
            high[:, head : head + HEAD_SIZE_DIM] = h
            low[:, head : head + HEAD_SIZE_DIM] = l

        pairs = [(part_refs[2 * i], part_refs[2 * i + 1]) for i in range(n_parts // 2)]
        attend(pairs, pairs[ask], q_width, kv_width, store)
    attended = (high[...], low[...])
    for k in range(outs[0].shape[1] // step):
        columns = slice(k * step, (k + 1) * step)
        if start is None:
            w = (w_high[:, columns], w_low[:, columns])
        else:
            copy(k).wait()
            w = split(buf[k])
        mixed = dot3(attended, w)
        at = 0
        for o in outs:
            o[:, columns] = mixed[at : at + o.shape[0]]
            at += o.shape[0]


def mix(operands, ask, rows, keyed, w, kv_width, slots, start, columns, name, step=512):
    q_width = w[0].shape[0]
    steps = columns // step
    attended = [jax.ShapeDtypeStruct((rows, q_width), jnp.bfloat16)] * (0 if ask is None else 2)
    out_shape = attended + [jax.ShapeDtypeStruct((s, columns), jnp.float32) for s in slots]
    vmem = pl.BlockSpec(memory_space=pltpu.VMEM)
    scratch = [pltpu.VMEM((steps, q_width, step), jnp.float32), pltpu.SemaphoreType.DMA((steps,))]
    return pl.pallas_call(
        functools.partial(mix_kernel, len(operands), ask, q_width, kv_width, start, step),
        in_specs=[vmem] * len(operands) + ([vmem] * 2 if start is None else [pl.BlockSpec(memory_space=pl.ANY)]),
        out_specs=[vmem] * len(out_shape),
        out_shape=out_shape,
        scratch_shapes=[] if start is None else scratch,
        compiler_params=pltpu.CompilerParams(vmem_limit_bytes=VMEM_LIMIT),
        cost_estimate=pl.CostEstimate(
            flops=6 * rows * q_width * columns + 24 * rows * keyed * q_width,
            bytes_accessed=4 * columns * (q_width + rows),
            transcendentals=rows * keyed * q_width // HEAD_SIZE_DIM,
        ),
        name=name,
    )(*operands, *w)


def attend_out(parts, first, last, w, kv_width, slots, columns):
    rows = sum(a.shape[0] for a, _ in parts[first:last])
    keyed = sum(a.shape[0] for a, _ in parts)
    flat = [r for pair in parts for r in pair]
    res = mix(flat, slice(first, last), rows, keyed, w, kv_width, slots, None, columns, "attend_out")
    return res[:2], res[2:]


def out_again(attended, w_out, slots, start, columns):
    rows = attended[0].shape[0]
    return mix(list(attended), None, rows, 0, [w_out], 0, slots, start, columns, "out_again")


def after(a, *others):
    return lax.optimization_barrier((a, *others))[0]


def cut(sizes):
    return [(sum(sizes[:i]), size) for i, size in enumerate(sizes)]


def on_line_of_four(tokens, w_query, w_key, w_value, w_out):
    rows, depth = tokens.shape
    weights = (w_query, w_key, w_value)
    kv_width = w_key.shape[1]
    halves = cut([depth // 2] * 2)
    last = cut([depth // 2, depth // 4, depth // 4])

    def hop(a, pairs):
        return lax.ppermute(a, "col", pairs)

    def swap(a):
        return lax.ppermute(a, "row", CORES)

    def columns(a, start, size):
        return a[:, start : start + size]

    own = [columns(tokens, *h) for h in halves]
    near = [hop(a, PAIRS) for a in own]
    mid = [hop(a, MIDDLE) for a in own]
    first = project([((own[0], 0),)], weights, *halves[0])
    near[1] = after(near[1], first)
    mid2 = [hop(a, MIDDLE) for a in near]
    end2 = [hop(a, ENDS_IN) for a in mid]
    first = project([((own[1], 0),)], weights, *halves[1], first)
    mid2[0] = after(mid2[0], first)
    pieces = cut([w_out.shape[1] // 2] * 2)
    w_split = halve(w_out, *pieces[0], first)
    second = third = None
    for c, h in enumerate(halves):
        block = [((near[c], 0),), ((mid[c], 0), (end2[c], 0))]
        second = project(block, weights, *h, second, before=w_split[:1])
        if c == 0:
            mid2[1] = after(mid2[1], second)
    first, second = [(a, swap(a)) for a in (first, second)]
    for i, (start, size) in enumerate(last):
        half = start // halves[0][1]
        at = start - halves[half][0]
        end3 = hop(columns(mid2[half], at, size) if size < halves[0][1] else mid2[half], ENDS_IN)
        block = ((mid2[half], at), (end3, 0))
        if i == len(last) - 1:
            third = project_last(block, kept, third)
        elif i == len(last) - 2:
            third, *kept = project([block], weights, start, size, third, last[-1][1])
        else:
            third = project([block], weights, start, size, third)
    third = (third, swap(third))

    parts = [first, second, third]
    a_third, m_third = attend_out(parts, 2, 3, w_split, kv_width, [rows], pieces[0][1])
    m_third = [m_third[0], out_again(a_third, w_out, [rows], *pieces[1])[0]]
    r1 = [hop(m, ENDS_OUT) for m in m_third]
    others = [tuple(after(a, *m_third) for a in first), second, third]
    a_rest, mixed = attend_out(others, 0, 2, w_split, kv_width, [rows] * 3, pieces[0][1])
    mixed = [mixed, out_again(a_rest, w_out, [rows] * 3, *pieces[1])]
    result = []
    for (m_own, m_near, m_second), m, r in zip(mixed, m_third, r1):
        r2e = hop(m_second, ENDS_OUT)
        r2m = hop(m + r, MIDDLE)
        r3m = hop(m_second + r2e, MIDDLE)
        r3x = hop(m_near + r2m, PAIRS)
        result.append(m_own + (r3x + r3m))
    return jnp.concatenate(result, axis=1)


def on_device(tokens, w_query, w_key, w_value, w_out):
    highest = lax.Precision.HIGHEST
    gathered = lax.all_gather(tokens, "col", axis=0, tiled=True)
    q_width = w_query.shape[1]
    kv_width = w_key.shape[1]

    def product(weight):
        return jnp.dot(gathered, weight, preferred_element_type=jnp.float32, precision=highest)

    joined = lax.psum_scatter(
        jnp.concatenate([product(w_query), product(w_key), product(w_value)], axis=1),
        "row",
        scatter_dimension=0,
        tiled=True,
    )
    query_rows = joined[:, :q_width]
    keys = lax.all_gather(joined[:, q_width : q_width + kv_width], "row", axis=0, tiled=True)
    values = lax.all_gather(joined[:, q_width + kv_width :], "row", axis=0, tiled=True)
    count_of_rows, count_of_heads = query_rows.shape[0], kv_width // HEAD_SIZE_DIM
    query_rows = query_rows.reshape(count_of_rows, count_of_heads, GROUP, HEAD_SIZE_DIM)
    keys = keys.reshape(-1, count_of_heads, HEAD_SIZE_DIM)
    values = values.reshape(-1, count_of_heads, HEAD_SIZE_DIM)
    scores = jnp.einsum("rkgd,nkd->kgrn", query_rows, keys, precision=highest)
    weights = jax.nn.softmax(scores * (1.0 / math.sqrt(HEAD_SIZE_DIM)), axis=-1)
    attended = jnp.einsum("kgrn,nkd->rkgd", weights, values, precision=highest)
    attended = lax.all_gather(attended.reshape(count_of_rows, q_width), "row", axis=0, tiled=True)
    return lax.psum_scatter(
        jnp.dot(attended, w_out, preferred_element_type=jnp.float32, precision=highest),
        "col",
        scatter_dimension=0,
        tiled=True,
    )


def solution(mesh):
    placed = (
        P(("depth", "col"), "row"),
        P("row", "col"),
        P("row", "col"),
        P("row", "col"),
        P("col", "row"),
    )
    here = mesh.shape["row"] == 2 and mesh.shape["col"] == 4
    return jax.shard_map(
        on_line_of_four if here else on_device,
        mesh=mesh,
        in_specs=placed,
        out_specs=P(("depth", "col"), "row"),
        check_vma=False,
    )
```

```python
import functools
import math

import jax
import jax.numpy as jnp
from jax import lax
from jax.experimental import pallas as pl
from jax.experimental.pallas import tpu as pltpu
from jax.sharding import PartitionSpec as P

QUERY_HEADS = 32
KEY_VALUE_HEADS = 4
HEAD_SIZE_DIM = 128
GROUP = QUERY_HEADS // KEY_VALUE_HEADS

VMEM_LIMIT = 38 * 1024 * 1024

ENDS_IN = [(1, 0), (2, 3)]
ENDS_OUT = [(0, 1), (3, 2)]
PAIRS = [(0, 1), (1, 0), (2, 3), (3, 2)]
MIDDLE = [(1, 2), (2, 1)]
CORES = [(0, 1), (1, 0)]


def split(a):
    high = a.astype(jnp.bfloat16)
    return high, (a - high.astype(jnp.float32)).astype(jnp.bfloat16)


def dot(a, b, dims=((1,), (0,))):
    return lax.dot_general(a, b, (dims, ((), ())), preferred_element_type=jnp.float32)


def dot_split(a, b):
    rows = a[0].shape[0]
    both = jnp.concatenate(a, axis=0)
    high, low = dot(both, b[0]), dot(both, b[1])
    return high[:rows] + ((high[rows:] + low[:rows]) + low[rows:])


def project_kernel(terms, with_total, first, steps, step, n_before, *refs):
    n_x = sum(len(t) for t in terms)
    x_refs, w_refs, rest = refs[:n_x], refs[n_x : n_x + 3], refs[n_x + 3 :]
    total, rest = rest[0], rest[(1 if with_total else 0) + n_before :]
    out, kept, bufs, sems = rest[0], rest[1:-4], rest[-4:-1], rest[-1]

    def copies(k):
        rows = pl.ds(first + k * step, step)
        return [pltpu.make_async_copy(w.at[rows], b.at[k], sems.at[k, i]) for i, (w, b) in enumerate(zip(w_refs, bufs))]

    for k in range(bufs[0].shape[0]):
        for c in copies(k):
            c.start()
    for k in range(steps):
        blocks, i = [], 0
        for term in terms:
            block = None
            for at in term:
                piece = x_refs[i][:, at + k * step : at + (k + 1) * step]
                block = piece if block is None else block + piece
                i += 1
            blocks.append(block)
        x = split(jnp.concatenate(blocks, axis=0) if len(blocks) > 1 else blocks[0])
        for c in copies(k):
            c.wait()
        offset = 0
        for b in bufs:
            width = b.shape[2]
            columns = slice(offset, offset + width)
            product = dot_split(x, split(b[k]))
            if k > 0:
                out[:, columns] += product
            elif with_total:
                out[:, columns] = total[:, columns] + product
            else:
                out[:, columns] = product
            offset += width
    for k in range(steps, bufs[0].shape[0]):
        for c in copies(k):
            c.wait()
        offset, rows = 0, slice((k - steps) * step, (k - steps + 1) * step)
        for b in bufs:
            columns = slice(offset, offset + b.shape[2])
            kept[0][rows, columns], kept[1][rows, columns] = split(b[k])
            offset += b.shape[2]


def project(blocks, weights, start, depth, total=None, keep=0, before=(), step=512):
    terms = tuple(tuple(at for _, at in b) for b in blocks)
    operands = [a for b in blocks for a, _ in b]
    rows = sum(b[0][0].shape[0] for b in blocks)
    width = sum(w.shape[1] for w in weights)
    steps = depth // step
    vmem, anywhere = pl.BlockSpec(memory_space=pltpu.VMEM), pl.BlockSpec(memory_space=pl.ANY)
    in_specs = [vmem] * len(operands) + [anywhere] * len(weights)
    operands += weights
    if total is not None:
        in_specs.append(vmem)
        operands.append(total)
    in_specs += [anywhere] * len(before)
    operands += before
    return pl.pallas_call(
        functools.partial(project_kernel, terms, total is not None, start, steps, step, len(before)),
        in_specs=in_specs,
        out_specs=[vmem] * 3 if keep else vmem,
        out_shape=[jax.ShapeDtypeStruct((rows, width), jnp.float32)]
        + [jax.ShapeDtypeStruct((keep, width), jnp.bfloat16)] * 2
        if keep
        else jax.ShapeDtypeStruct((rows, width), jnp.float32),
        scratch_shapes=[pltpu.VMEM((steps + keep // step, step, w.shape[1]), jnp.float32) for w in weights]
        + [pltpu.SemaphoreType.DMA((steps + keep // step, len(weights)))],
        compiler_params=pltpu.CompilerParams(vmem_limit_bytes=VMEM_LIMIT),
        cost_estimate=pl.CostEstimate(
            flops=8 * rows * depth * width, bytes_accessed=4 * depth * (rows + width), transcendentals=0
        ),
        name="project",
    )(*operands)


def project_last_kernel(at, x, y, high, low, total, out):
    size = y.shape[1]
    block = split(x[:, at : at + size] + y[...])
    out[...] = total[...] + dot_split(block, (high[...], low[...]))


def project_last(block, kept, total):
    (x, at), (y, _) = block
    vmem = pl.BlockSpec(memory_space=pltpu.VMEM)
    return pl.pallas_call(
        functools.partial(project_last_kernel, at),
        in_specs=[vmem] * 5,
        out_specs=vmem,
        out_shape=jax.ShapeDtypeStruct(total.shape, jnp.float32),
        compiler_params=pltpu.CompilerParams(vmem_limit_bytes=VMEM_LIMIT),
        cost_estimate=pl.CostEstimate(
            flops=8 * y.shape[1] * total.size, bytes_accessed=4 * y.shape[1] * total.shape[1], transcendentals=0
        ),
        name="project_last",
    )(x, y, *kept, total)


def attend(keyed, asked, q_width, kv_width, store):
    groups = kv_width // HEAD_SIZE_DIM
    scale = 1.0 / math.sqrt(HEAD_SIZE_DIM)

    def columns(pairs, start):
        stop = start + HEAD_SIZE_DIM
        return jnp.concatenate([a[:, start:stop] + b[:, start:stop] for a, b in pairs], axis=0)

    rows = sum(a.shape[0] for a, _ in asked)
    together = GROUP if rows <= 64 else 1
    for g in range(groups):
        at = q_width + g * HEAD_SIZE_DIM
        k_high, k_low = split(columns(keyed, at))
        v_high, v_low = split(columns(keyed, at + kv_width))
        k_highs = jnp.concatenate([k_high, k_high], axis=1)
        k_lows = jnp.concatenate([k_low, k_low], axis=1)
        v_both = jnp.concatenate([v_high, v_low], axis=1)
        for j in range(0, GROUP, together):
            heads = [(g * GROUP + j + i) * HEAD_SIZE_DIM for i in range(together)]
            queries = split(jnp.concatenate([columns(asked, h) for h in heads], axis=0) * scale)
            q_both = jnp.concatenate(queries, axis=1)
            scores = dot(q_both, k_highs, ((1,), (1,))) + dot(q_both, k_lows, ((1,), (1,)))
            weights = jnp.exp(scores - jnp.max(scores, axis=-1, keepdims=True))
            total = jnp.sum(weights, axis=-1, keepdims=True)
            p_high, p_low = split(weights)
            both = dot(p_high, v_both)
            less = dot(p_low, v_both)
            result = both[:, :HEAD_SIZE_DIM] + (
                (both[:, HEAD_SIZE_DIM:] + less[:, :HEAD_SIZE_DIM]) + less[:, HEAD_SIZE_DIM:]
            )
            result = result / total
            for i, h in enumerate(heads):
                store(h, result[i * rows : (i + 1) * rows])


def halve_kernel(start, w_ref, before, high, low, buf, sems):
    steps, step, size = buf.shape

    def copy(k):
        return pltpu.make_async_copy(w_ref.at[pl.ds(k * step, step), pl.ds(start, size)], buf.at[k], sems.at[k])

    for k in range(steps):
        copy(k).start()
    for k in range(steps):
        copy(k).wait()
        rows = slice(k * step, (k + 1) * step)
        high[rows], low[rows] = split(buf[k])


def halve(w, start, size, before, step=256):
    steps = w.shape[0] // step
    vmem, anywhere = pl.BlockSpec(memory_space=pltpu.VMEM), pl.BlockSpec(memory_space=pl.ANY)
    return pl.pallas_call(
        functools.partial(halve_kernel, start),
        in_specs=[anywhere] * 2,
        out_specs=[vmem] * 2,
        out_shape=[jax.ShapeDtypeStruct((w.shape[0], size), jnp.bfloat16)] * 2,
        scratch_shapes=[pltpu.VMEM((steps, step, size), jnp.float32), pltpu.SemaphoreType.DMA((steps,))],
        compiler_params=pltpu.CompilerParams(vmem_limit_bytes=VMEM_LIMIT),
        cost_estimate=pl.CostEstimate(flops=w.shape[0] * size, bytes_accessed=8 * w.shape[0] * size, transcendentals=0),
        name="halve",
    )(w, before)


def mix_kernel(n_parts, ask, q_width, kv_width, start, step, *refs):
    part_refs, rest = refs[:n_parts], refs[n_parts:]
    if start is None:
        (w_high, w_low), outs = rest[:2], rest[2:]
    else:
        w_ref, outs, (buf, sems) = rest[0], rest[1:-2], rest[-2:]

        def copy(k):
            return pltpu.make_async_copy(w_ref.at[:, pl.ds(start + k * step, step)], buf.at[k], sems.at[k])

        for k in range(buf.shape[0]):
            copy(k).start()
    if ask is None:
        high, low = part_refs
    else:
        high, low, outs = outs[0], outs[1], outs[2:]

        def store(head, rows):
            h, l = split(rows)
            high[:, head : head + HEAD_SIZE_DIM] = h
            low[:, head : head + HEAD_SIZE_DIM] = l

        pairs = [(part_refs[2 * i], part_refs[2 * i + 1]) for i in range(n_parts // 2)]
        attend(pairs, pairs[ask], q_width, kv_width, store)
    attended = (high[...], low[...])
    for k in range(outs[0].shape[1] // step):
        columns = slice(k * step, (k + 1) * step)
        if start is None:
            w = (w_high[:, columns], w_low[:, columns])
        else:
            copy(k).wait()
            w = split(buf[k])
        mixed = dot_split(attended, w)
        at = 0
        for o in outs:
            o[:, columns] = mixed[at : at + o.shape[0]]
            at += o.shape[0]


def mix(operands, ask, rows, keyed, w, kv_width, slots, start, columns, name, step=512):
    q_width = w[0].shape[0]
    steps = columns // step
    attended = [jax.ShapeDtypeStruct((rows, q_width), jnp.bfloat16)] * (0 if ask is None else 2)
    out_shape = attended + [jax.ShapeDtypeStruct((s, columns), jnp.float32) for s in slots]
    vmem = pl.BlockSpec(memory_space=pltpu.VMEM)
    scratch = [pltpu.VMEM((steps, q_width, step), jnp.float32), pltpu.SemaphoreType.DMA((steps,))]
    return pl.pallas_call(
        functools.partial(mix_kernel, len(operands), ask, q_width, kv_width, start, step),
        in_specs=[vmem] * len(operands) + ([vmem] * 2 if start is None else [pl.BlockSpec(memory_space=pl.ANY)]),
        out_specs=[vmem] * len(out_shape),
        out_shape=out_shape,
        scratch_shapes=[] if start is None else scratch,
        compiler_params=pltpu.CompilerParams(vmem_limit_bytes=VMEM_LIMIT),
        cost_estimate=pl.CostEstimate(
            flops=8 * rows * q_width * columns + 32 * rows * keyed * q_width,
            bytes_accessed=4 * columns * (q_width + rows),
            transcendentals=rows * keyed * q_width // HEAD_SIZE_DIM,
        ),
        name=name,
    )(*operands, *w)


def attend_out(parts, first, last, w, kv_width, slots, columns):
    rows = sum(a.shape[0] for a, _ in parts[first:last])
    keyed = sum(a.shape[0] for a, _ in parts)
    flat = [r for pair in parts for r in pair]
    res = mix(flat, slice(first, last), rows, keyed, w, kv_width, slots, None, columns, "attend_out")
    return res[:2], res[2:]


def out_again(attended, w_out, slots, start, columns):
    rows = attended[0].shape[0]
    return mix(list(attended), None, rows, 0, [w_out], 0, slots, start, columns, "out_again")


def after(a, *others):
    return lax.optimization_barrier((a, *others))[0]


def cut(sizes):
    return [(sum(sizes[:i]), size) for i, size in enumerate(sizes)]


def on_line_of_four(tokens, w_query, w_key, w_value, w_out):
    rows, depth = tokens.shape
    weights = (w_query, w_key, w_value)
    kv_width = w_key.shape[1]
    halves = cut([depth // 2] * 2)
    last = cut([depth // 2, depth // 4, depth // 4])

    def hop(a, pairs):
        return lax.ppermute(a, "col", pairs)

    def swap(a):
        return lax.ppermute(a, "row", CORES)

    def columns(a, start, size):
        return a[:, start : start + size]

    own = [columns(tokens, *halves[0])]
    own.append(columns(after(tokens, own[0]), *halves[1]))
    near = [hop(a, PAIRS) for a in own]
    mid = [hop(a, MIDDLE) for a in own]
    first = project([((own[0], 0),)], weights, *halves[0])
    near[1] = after(near[1], first)
    mid2 = [hop(a, MIDDLE) for a in near]
    end2 = [hop(a, ENDS_IN) for a in mid]
    first = project([((own[1], 0),)], weights, *halves[1], first)
    mid2[0] = after(mid2[0], first)
    pieces = cut([w_out.shape[1] // 2] * 2)
    w_split = halve(w_out, *pieces[0], first)
    second = third = None
    for c, h in enumerate(halves):
        block = [((near[c], 0),), ((mid[c], 0), (end2[c], 0))]
        second = project(block, weights, *h, second, before=w_split[:1])
        if c == 0:
            mid2[1] = after(mid2[1], second)
    first, second = [(a, swap(a)) for a in (first, second)]
    for i, (start, size) in enumerate(last):
        half = start // halves[0][1]
        at = start - halves[half][0]
        end3 = hop(columns(mid2[half], at, size) if size < halves[0][1] else mid2[half], ENDS_IN)
        block = ((mid2[half], at), (end3, 0))
        if i == len(last) - 1:
            third = project_last(block, kept, third)
        elif i == len(last) - 2:
            third, *kept = project([block], weights, start, size, third, last[-1][1])
        else:
            third = project([block], weights, start, size, third)
    third = (third, swap(third))

    parts = [first, second, third]
    a_third, m_third = attend_out(parts, 2, 3, w_split, kv_width, [rows], pieces[0][1])
    m_third = [m_third[0], out_again(a_third, w_out, [rows], *pieces[1])[0]]
    r1 = [hop(m, ENDS_OUT) for m in m_third]
    others = [tuple(after(a, *m_third) for a in first), second, third]
    a_rest, mixed = attend_out(others, 0, 2, w_split, kv_width, [rows] * 3, pieces[0][1])
    mixed = [mixed, out_again(a_rest, w_out, [rows] * 3, *pieces[1])]
    result = []
    for (m_own, m_near, m_second), m, r in zip(mixed, m_third, r1):
        r2e = hop(m_second, ENDS_OUT)
        r2m = hop(m + r, MIDDLE)
        r3m = hop(m_second + r2e, MIDDLE)
        r3x = hop(m_near + r2m, PAIRS)
        result.append(m_own + (r3x + r3m))
    return jnp.concatenate(result, axis=1)


def on_device(tokens, w_query, w_key, w_value, w_out):
    highest = lax.Precision.HIGHEST
    gathered = lax.all_gather(tokens, "col", axis=0, tiled=True)
    q_width = w_query.shape[1]
    kv_width = w_key.shape[1]

    def product(weight):
        return jnp.dot(gathered, weight, preferred_element_type=jnp.float32, precision=highest)

    joined = lax.psum_scatter(
        jnp.concatenate([product(w_query), product(w_key), product(w_value)], axis=1),
        "row",
        scatter_dimension=0,
        tiled=True,
    )
    query_rows = joined[:, :q_width]
    keys = lax.all_gather(joined[:, q_width : q_width + kv_width], "row", axis=0, tiled=True)
    values = lax.all_gather(joined[:, q_width + kv_width :], "row", axis=0, tiled=True)
    count_of_rows, count_of_heads = query_rows.shape[0], kv_width // HEAD_SIZE_DIM
    query_rows = query_rows.reshape(count_of_rows, count_of_heads, GROUP, HEAD_SIZE_DIM)
    keys = keys.reshape(-1, count_of_heads, HEAD_SIZE_DIM)
    values = values.reshape(-1, count_of_heads, HEAD_SIZE_DIM)
    scores = jnp.einsum("rkgd,nkd->kgrn", query_rows, keys, precision=highest)
    weights = jax.nn.softmax(scores * (1.0 / math.sqrt(HEAD_SIZE_DIM)), axis=-1)
    attended = jnp.einsum("kgrn,nkd->rkgd", weights, values, precision=highest)
    attended = lax.all_gather(attended.reshape(count_of_rows, q_width), "row", axis=0, tiled=True)
    return lax.psum_scatter(
        jnp.dot(attended, w_out, preferred_element_type=jnp.float32, precision=highest),
        "col",
        scatter_dimension=0,
        tiled=True,
    )


def solution(mesh):
    placed = (
        P(("depth", "col"), "row"),
        P("row", "col"),
        P("row", "col"),
        P("row", "col"),
        P("col", "row"),
    )
    here = mesh.shape["row"] == 2 and mesh.shape["col"] == 4
    return jax.shard_map(
        on_line_of_four if here else on_device,
        mesh=mesh,
        in_specs=placed,
        out_specs=P(("depth", "col"), "row"),
        check_vma=False,
    )
```

```python
import functools
import math

import jax
import jax.numpy as jnp
from jax import lax
from jax.experimental import pallas as pl
from jax.experimental.pallas import tpu as pltpu
from jax.sharding import PartitionSpec as P

QUERY_HEADS = 32
KEY_VALUE_HEADS = 4
HEAD_SIZE_DIM = 128
GROUP = QUERY_HEADS // KEY_VALUE_HEADS

VMEM_LIMIT = 38 * 1024 * 1024

ENDS_IN = [(1, 0), (2, 3)]
ENDS_OUT = [(0, 1), (3, 2)]
PAIRS = [(0, 1), (1, 0), (2, 3), (3, 2)]
MIDDLE = [(1, 2), (2, 1)]
CORES = [(0, 1), (1, 0)]


def split(a):
    high = a.astype(jnp.bfloat16)
    return high, (a - high.astype(jnp.float32)).astype(jnp.bfloat16)


def dot(a, b, dims=((1,), (0,))):
    return lax.dot_general(a, b, (dims, ((), ())), preferred_element_type=jnp.float32)


def dot_split(a, b):
    rows = a[0].shape[0]
    both = jnp.concatenate(a, axis=0)
    high, low = dot(both, b[0]), dot(both, b[1])
    return high[:rows] + ((high[rows:] + low[:rows]) + low[rows:])


def project_kernel(terms, with_total, first, steps, step, n_before, *refs):
    n_x = sum(len(t) for t in terms)
    x_refs, w_refs, rest = refs[:n_x], refs[n_x : n_x + 3], refs[n_x + 3 :]
    total, rest = rest[0], rest[(1 if with_total else 0) + n_before :]
    out, kept, bufs, sems = rest[0], rest[1:-4], rest[-4:-1], rest[-1]

    def copies(k):
        rows = pl.ds(first + k * step, step)
        return [pltpu.make_async_copy(w.at[rows], b.at[k], sems.at[k, i]) for i, (w, b) in enumerate(zip(w_refs, bufs))]

    for k in range(bufs[0].shape[0]):
        for c in copies(k):
            c.start()
    for k in range(steps):
        blocks, i = [], 0
        for term in terms:
            block = None
            for at in term:
                piece = x_refs[i][:, at + k * step : at + (k + 1) * step]
                block = piece if block is None else block + piece
                i += 1
            blocks.append(block)
        x = split(jnp.concatenate(blocks, axis=0) if len(blocks) > 1 else blocks[0])
        for c in copies(k):
            c.wait()
        offset = 0
        for b in bufs:
            width = b.shape[2]
            columns = slice(offset, offset + width)
            product = dot_split(x, split(b[k]))
            if k > 0:
                out[:, columns] += product
            elif with_total:
                out[:, columns] = total[:, columns] + product
            else:
                out[:, columns] = product
            offset += width
    for k in range(steps, bufs[0].shape[0]):
        for c in copies(k):
            c.wait()
        offset, rows = 0, slice((k - steps) * step, (k - steps + 1) * step)
        for b in bufs:
            columns = slice(offset, offset + b.shape[2])
            kept[0][rows, columns], kept[1][rows, columns] = split(b[k])
            offset += b.shape[2]


def project(blocks, weights, start, depth, total=None, keep=0, before=(), step=512):
    terms = tuple(tuple(at for _, at in b) for b in blocks)
    operands = [a for b in blocks for a, _ in b]
    rows = sum(b[0][0].shape[0] for b in blocks)
    width = sum(w.shape[1] for w in weights)
    steps = depth // step
    vmem, anywhere = pl.BlockSpec(memory_space=pltpu.VMEM), pl.BlockSpec(memory_space=pl.ANY)
    in_specs = [vmem] * len(operands) + [anywhere] * len(weights)
    operands += weights
    if total is not None:
        in_specs.append(vmem)
        operands.append(total)
    in_specs += [anywhere] * len(before)
    operands += before
    return pl.pallas_call(
        functools.partial(project_kernel, terms, total is not None, start, steps, step, len(before)),
        in_specs=in_specs,
        out_specs=[vmem] * 3 if keep else vmem,
        out_shape=[jax.ShapeDtypeStruct((rows, width), jnp.float32)]
        + [jax.ShapeDtypeStruct((keep, width), jnp.bfloat16)] * 2
        if keep
        else jax.ShapeDtypeStruct((rows, width), jnp.float32),
        scratch_shapes=[pltpu.VMEM((steps + keep // step, step, w.shape[1]), jnp.float32) for w in weights]
        + [pltpu.SemaphoreType.DMA((steps + keep // step, len(weights)))],
        compiler_params=pltpu.CompilerParams(vmem_limit_bytes=VMEM_LIMIT),
        cost_estimate=pl.CostEstimate(
            flops=8 * rows * depth * width, bytes_accessed=4 * depth * (rows + width), transcendentals=0
        ),
        name="project",
    )(*operands)


def project_last_kernel(at, x, y, high, low, total, out):
    size = y.shape[1]
    block = split(x[:, at : at + size] + y[...])
    out[...] = total[...] + dot_split(block, (high[...], low[...]))


def project_last(block, kept, total):
    (x, at), (y, _) = block
    vmem = pl.BlockSpec(memory_space=pltpu.VMEM)
    return pl.pallas_call(
        functools.partial(project_last_kernel, at),
        in_specs=[vmem] * 5,
        out_specs=vmem,
        out_shape=jax.ShapeDtypeStruct(total.shape, jnp.float32),
        compiler_params=pltpu.CompilerParams(vmem_limit_bytes=VMEM_LIMIT),
        cost_estimate=pl.CostEstimate(
            flops=8 * y.shape[1] * total.size, bytes_accessed=4 * y.shape[1] * total.shape[1], transcendentals=0
        ),
        name="project_last",
    )(x, y, *kept, total)


def attend(keyed, asked, q_width, kv_width, store):
    groups = kv_width // HEAD_SIZE_DIM
    scale = 1.0 / math.sqrt(HEAD_SIZE_DIM)

    def columns(pairs, start):
        stop = start + HEAD_SIZE_DIM
        return jnp.concatenate([a[:, start:stop] + b[:, start:stop] for a, b in pairs], axis=0)

    rows = sum(a.shape[0] for a, _ in asked)
    together = GROUP if rows <= 64 else 1
    for g in range(groups):
        at = q_width + g * HEAD_SIZE_DIM
        k_high, k_low = split(columns(keyed, at))
        v_high, v_low = split(columns(keyed, at + kv_width))
        k_highs = jnp.concatenate([k_high, k_high], axis=1)
        k_lows = jnp.concatenate([k_low, k_low], axis=1)
        v_both = jnp.concatenate([v_high, v_low], axis=1)
        for j in range(0, GROUP, together):
            heads = [(g * GROUP + j + i) * HEAD_SIZE_DIM for i in range(together)]
            queries = split(jnp.concatenate([columns(asked, h) for h in heads], axis=0) * scale)
            q_both = jnp.concatenate(queries, axis=1)
            scores = dot(q_both, k_highs, ((1,), (1,))) + dot(q_both, k_lows, ((1,), (1,)))
            weights = jnp.exp(scores - jnp.max(scores, axis=-1, keepdims=True))
            total = jnp.sum(weights, axis=-1, keepdims=True)
            p_high, p_low = split(weights)
            both = dot(p_high, v_both)
            less = dot(p_low, v_both)
            result = both[:, :HEAD_SIZE_DIM] + (
                (both[:, HEAD_SIZE_DIM:] + less[:, :HEAD_SIZE_DIM]) + less[:, HEAD_SIZE_DIM:]
            )
            result = result / total
            for i, h in enumerate(heads):
                store(h, result[i * rows : (i + 1) * rows])


def halve_kernel(start, w_ref, before, high, low, buf, sems):
    steps, step, size = buf.shape

    def copy(k):
        return pltpu.make_async_copy(w_ref.at[pl.ds(k * step, step), pl.ds(start, size)], buf.at[k], sems.at[k])

    for k in range(steps):
        copy(k).start()
    for k in range(steps):
        copy(k).wait()
        rows = slice(k * step, (k + 1) * step)
        high[rows], low[rows] = split(buf[k])


def halve(w, start, size, before, step=256):
    steps = w.shape[0] // step
    vmem, anywhere = pl.BlockSpec(memory_space=pltpu.VMEM), pl.BlockSpec(memory_space=pl.ANY)
    return pl.pallas_call(
        functools.partial(halve_kernel, start),
        in_specs=[anywhere] * 2,
        out_specs=[vmem] * 2,
        out_shape=[jax.ShapeDtypeStruct((w.shape[0], size), jnp.bfloat16)] * 2,
        scratch_shapes=[pltpu.VMEM((steps, step, size), jnp.float32), pltpu.SemaphoreType.DMA((steps,))],
        compiler_params=pltpu.CompilerParams(vmem_limit_bytes=VMEM_LIMIT),
        cost_estimate=pl.CostEstimate(flops=w.shape[0] * size, bytes_accessed=8 * w.shape[0] * size, transcendentals=0),
        name="halve",
    )(w, before)


def mix_kernel(n_parts, ask, q_width, kv_width, start, step, *refs):
    part_refs, rest = refs[:n_parts], refs[n_parts:]
    if start is None:
        (w_high, w_low), outs = rest[:2], rest[2:]
    else:
        w_ref, outs, (buf, sems) = rest[0], rest[1:-2], rest[-2:]

        def copy(k):
            return pltpu.make_async_copy(w_ref.at[:, pl.ds(start + k * step, step)], buf.at[k], sems.at[k])

        for k in range(buf.shape[0]):
            copy(k).start()
    if ask is None:
        high, low = part_refs
    else:
        high, low, outs = outs[0], outs[1], outs[2:]

        def store(head, rows):
            h, l = split(rows)
            high[:, head : head + HEAD_SIZE_DIM] = h
            low[:, head : head + HEAD_SIZE_DIM] = l

        pairs = [(part_refs[2 * i], part_refs[2 * i + 1]) for i in range(n_parts // 2)]
        attend(pairs, pairs[ask], q_width, kv_width, store)
    attended = (high[...], low[...])
    for k in range(outs[0].shape[1] // step):
        columns = slice(k * step, (k + 1) * step)
        if start is None:
            w = (w_high[:, columns], w_low[:, columns])
        else:
            copy(k).wait()
            w = split(buf[k])
        mixed = dot_split(attended, w)
        at = 0
        for o in outs:
            o[:, columns] = mixed[at : at + o.shape[0]]
            at += o.shape[0]


def mix(operands, ask, rows, keyed, w, kv_width, slots, start, columns, name, step=512):
    q_width = w[0].shape[0]
    steps = columns // step
    attended = [jax.ShapeDtypeStruct((rows, q_width), jnp.bfloat16)] * (0 if ask is None else 2)
    out_shape = attended + [jax.ShapeDtypeStruct((s, columns), jnp.float32) for s in slots]
    vmem = pl.BlockSpec(memory_space=pltpu.VMEM)
    scratch = [pltpu.VMEM((steps, q_width, step), jnp.float32), pltpu.SemaphoreType.DMA((steps,))]
    return pl.pallas_call(
        functools.partial(mix_kernel, len(operands), ask, q_width, kv_width, start, step),
        in_specs=[vmem] * len(operands) + ([vmem] * 2 if start is None else [pl.BlockSpec(memory_space=pl.ANY)]),
        out_specs=[vmem] * len(out_shape),
        out_shape=out_shape,
        scratch_shapes=[] if start is None else scratch,
        compiler_params=pltpu.CompilerParams(vmem_limit_bytes=VMEM_LIMIT),
        cost_estimate=pl.CostEstimate(
            flops=8 * rows * q_width * columns + 32 * rows * keyed * q_width,
            bytes_accessed=4 * columns * (q_width + rows),
            transcendentals=rows * keyed * q_width // HEAD_SIZE_DIM,
        ),
        name=name,
    )(*operands, *w)


def attend_out(parts, first, last, w, kv_width, slots, columns):
    rows = sum(a.shape[0] for a, _ in parts[first:last])
    keyed = sum(a.shape[0] for a, _ in parts)
    flat = [r for pair in parts for r in pair]
    res = mix(flat, slice(first, last), rows, keyed, w, kv_width, slots, None, columns, "attend_out")
    return res[:2], res[2:]


def out_again(attended, w_out, slots, start, columns):
    rows = attended[0].shape[0]
    return mix(list(attended), None, rows, 0, [w_out], 0, slots, start, columns, "out_again")


def after(a, *others):
    return lax.optimization_barrier((a, *others))[0]


def cut(sizes):
    return [(sum(sizes[:i]), size) for i, size in enumerate(sizes)]


def on_line_of_four(tokens, w_query, w_key, w_value, w_out):
    rows, depth = tokens.shape
    weights = (w_query, w_key, w_value)
    kv_width = w_key.shape[1]
    halves = cut([depth // 2] * 2)
    last = cut([depth // 2, depth // 4, depth // 4])

    def hop(a, pairs):
        return lax.ppermute(a, "col", pairs)

    def swap(a):
        return lax.ppermute(a, "row", CORES)

    def columns(a, start, size):
        return a[:, start : start + size]

    near = hop(tokens, PAIRS)
    mid = [hop(columns(tokens, *h), MIDDLE) for h in halves]
    first = project([((tokens, 0),)], weights, *halves[0])
    mid[0] = after(mid[0], first)
    end2 = [hop(a, ENDS_IN) for a in mid]
    first = project([((tokens, halves[1][0]),)], weights, *halves[1], first, before=mid[:1])
    near = after(near, first)
    mid2 = [hop(columns(near, *halves[0]), MIDDLE)]
    pieces = cut([w_out.shape[1] // 2] * 2)
    w_split = halve(w_out, *pieces[0], near)
    second = third = None
    for (start, size), m, e in zip(halves, mid, end2):
        block = [((near, start),), ((m, 0), (e, 0))]
        second = project(block, weights, start, size, second, before=[w_split[0], mid[1]])
        if start == 0:
            mid2.append(hop(columns(after(near, w_split[0]), *halves[1]), MIDDLE))
            mid2[0] = after(mid2[0], second)
    first, second = [(a, swap(a)) for a in (first, second)]
    for i, (start, size) in enumerate(last):
        half = start // halves[0][1]
        at = start - halves[half][0]
        far = columns(mid2[half], at, size) if size < halves[0][1] else mid2[half]
        if i == 1:
            far = after(far, second[0])
        end3 = hop(far, ENDS_IN)
        block = ((mid2[half], at), (end3, 0))
        if i == len(last) - 1:
            third = project_last(block, kept, third)
        elif i == len(last) - 2:
            third, *kept = project([block], weights, start, size, third, last[-1][1])
        else:
            third = project([block], weights, start, size, third)
    third = (third, swap(third))

    parts = [first, second, third]
    a_third, m_third = attend_out(parts, 2, 3, w_split, kv_width, [rows], pieces[0][1])
    m_third = [m_third[0], out_again(a_third, w_out, [rows], *pieces[1])[0]]
    r1 = [hop(m, ENDS_OUT) for m in m_third]
    others = [tuple(after(a, *m_third) for a in first), second, third]
    a_rest, mixed = attend_out(others, 0, 2, w_split, kv_width, [rows] * 3, pieces[0][1])
    mixed = [mixed, out_again(a_rest, w_out, [rows] * 3, *pieces[1])]
    result = []
    for (m_own, m_near, m_second), m, r in zip(mixed, m_third, r1):
        r2e = hop(m_second, ENDS_OUT)
        r2m = hop(m + r, MIDDLE)
        r3m = hop(m_second + r2e, MIDDLE)
        r3x = hop(m_near + r2m, PAIRS)
        result.append(m_own + (r3x + r3m))
    return jnp.concatenate(result, axis=1)


def on_device(tokens, w_query, w_key, w_value, w_out):
    highest = lax.Precision.HIGHEST
    gathered = lax.all_gather(tokens, "col", axis=0, tiled=True)
    q_width = w_query.shape[1]
    kv_width = w_key.shape[1]

    def product(weight):
        return jnp.dot(gathered, weight, preferred_element_type=jnp.float32, precision=highest)

    joined = lax.psum_scatter(
        jnp.concatenate([product(w_query), product(w_key), product(w_value)], axis=1),
        "row",
        scatter_dimension=0,
        tiled=True,
    )
    query_rows = joined[:, :q_width]
    keys = lax.all_gather(joined[:, q_width : q_width + kv_width], "row", axis=0, tiled=True)
    values = lax.all_gather(joined[:, q_width + kv_width :], "row", axis=0, tiled=True)
    count_of_rows, count_of_heads = query_rows.shape[0], kv_width // HEAD_SIZE_DIM
    query_rows = query_rows.reshape(count_of_rows, count_of_heads, GROUP, HEAD_SIZE_DIM)
    keys = keys.reshape(-1, count_of_heads, HEAD_SIZE_DIM)
    values = values.reshape(-1, count_of_heads, HEAD_SIZE_DIM)
    scores = jnp.einsum("rkgd,nkd->kgrn", query_rows, keys, precision=highest)
    weights = jax.nn.softmax(scores * (1.0 / math.sqrt(HEAD_SIZE_DIM)), axis=-1)
    attended = jnp.einsum("kgrn,nkd->rkgd", weights, values, precision=highest)
    attended = lax.all_gather(attended.reshape(count_of_rows, q_width), "row", axis=0, tiled=True)
    return lax.psum_scatter(
        jnp.dot(attended, w_out, preferred_element_type=jnp.float32, precision=highest),
        "col",
        scatter_dimension=0,
        tiled=True,
    )


def solution(mesh):
    placed = (
        P(("depth", "col"), "row"),
        P("row", "col"),
        P("row", "col"),
        P("row", "col"),
        P("col", "row"),
    )
    here = mesh.shape["row"] == 2 and mesh.shape["col"] == 4
    return jax.shard_map(
        on_line_of_four if here else on_device,
        mesh=mesh,
        in_specs=placed,
        out_specs=P(("depth", "col"), "row"),
        check_vma=False,
    )
```

```python
import functools
import math

import jax
import jax.numpy as jnp
from jax import lax
from jax.experimental import pallas as pl
from jax.experimental.pallas import tpu as pltpu
from jax.sharding import PartitionSpec as P

QUERY_HEADS = 32
KEY_VALUE_HEADS = 4
HEAD_SIZE_DIM = 128
GROUP = QUERY_HEADS // KEY_VALUE_HEADS

VMEM_LIMIT = 38 * 1024 * 1024

ENDS_IN = [(1, 0), (2, 3)]
ENDS_OUT = [(0, 1), (3, 2)]
PAIRS = [(0, 1), (1, 0), (2, 3), (3, 2)]
MIDDLE = [(1, 2), (2, 1)]
CORES = [(0, 1), (1, 0)]


def split(a):
    high = a.astype(jnp.bfloat16)
    return high, (a - high.astype(jnp.float32)).astype(jnp.bfloat16)


def dot(a, b, dims=((1,), (0,))):
    return lax.dot_general(a, b, (dims, ((), ())), preferred_element_type=jnp.float32)


def dot_split(a, b):
    rows = a[0].shape[0]
    both = jnp.concatenate(a, axis=0)
    high, low = dot(both, b[0]), dot(both, b[1])
    return high[:rows] + ((high[rows:] + low[:rows]) + low[rows:])


def project_kernel(terms, with_total, first, steps, step, n_before, *refs):
    n_x = sum(len(t) for t in terms)
    x_refs, w_refs, rest = refs[:n_x], refs[n_x : n_x + 3], refs[n_x + 3 :]
    total, rest = rest[0], rest[(1 if with_total else 0) + n_before :]
    out, kept, bufs, sems = rest[0], rest[1:-4], rest[-4:-1], rest[-1]

    def copies(k):
        rows = pl.ds(first + k * step, step)
        return [pltpu.make_async_copy(w.at[rows], b.at[k], sems.at[k, i]) for i, (w, b) in enumerate(zip(w_refs, bufs))]

    for k in range(bufs[0].shape[0]):
        for c in copies(k):
            c.start()
    for k in range(steps):
        blocks, i = [], 0
        for term in terms:
            block = None
            for at in term:
                piece = x_refs[i][:, at + k * step : at + (k + 1) * step]
                block = piece if block is None else block + piece
                i += 1
            blocks.append(block)
        x = split(jnp.concatenate(blocks, axis=0) if len(blocks) > 1 else blocks[0])
        for c in copies(k):
            c.wait()
        offset = 0
        for b in bufs:
            width = b.shape[2]
            columns = slice(offset, offset + width)
            product = dot_split(x, split(b[k]))
            if k > 0:
                out[:, columns] += product
            elif with_total:
                out[:, columns] = total[:, columns] + product
            else:
                out[:, columns] = product
            offset += width
    for k in range(steps, bufs[0].shape[0]):
        for c in copies(k):
            c.wait()
        offset, rows = 0, slice((k - steps) * step, (k - steps + 1) * step)
        for b in bufs:
            columns = slice(offset, offset + b.shape[2])
            kept[0][rows, columns], kept[1][rows, columns] = split(b[k])
            offset += b.shape[2]


def project(blocks, weights, start, depth, total=None, keep=0, before=(), step=512):
    terms = tuple(tuple(at for _, at in b) for b in blocks)
    operands = [a for b in blocks for a, _ in b]
    rows = sum(b[0][0].shape[0] for b in blocks)
    width = sum(w.shape[1] for w in weights)
    steps = depth // step
    vmem, anywhere = pl.BlockSpec(memory_space=pltpu.VMEM), pl.BlockSpec(memory_space=pl.ANY)
    in_specs = [vmem] * len(operands) + [anywhere] * len(weights)
    operands += weights
    if total is not None:
        in_specs.append(vmem)
        operands.append(total)
    in_specs += [anywhere] * len(before)
    operands += before
    return pl.pallas_call(
        functools.partial(project_kernel, terms, total is not None, start, steps, step, len(before)),
        in_specs=in_specs,
        out_specs=[vmem] * 3 if keep else vmem,
        out_shape=[jax.ShapeDtypeStruct((rows, width), jnp.float32)]
        + [jax.ShapeDtypeStruct((keep, width), jnp.bfloat16)] * 2
        if keep
        else jax.ShapeDtypeStruct((rows, width), jnp.float32),
        scratch_shapes=[pltpu.VMEM((steps + keep // step, step, w.shape[1]), jnp.float32) for w in weights]
        + [pltpu.SemaphoreType.DMA((steps + keep // step, len(weights)))],
        compiler_params=pltpu.CompilerParams(vmem_limit_bytes=VMEM_LIMIT),
        cost_estimate=pl.CostEstimate(
            flops=8 * rows * depth * width, bytes_accessed=4 * depth * (rows + width), transcendentals=0
        ),
        name="project",
    )(*operands)


def project_last_kernel(at, x, y, high, low, total, out):
    size = y.shape[1]
    block = split(x[:, at : at + size] + y[...])
    out[...] = total[...] + dot_split(block, (high[...], low[...]))


def project_last(block, kept, total):
    (x, at), (y, _) = block
    vmem = pl.BlockSpec(memory_space=pltpu.VMEM)
    return pl.pallas_call(
        functools.partial(project_last_kernel, at),
        in_specs=[vmem] * 5,
        out_specs=vmem,
        out_shape=jax.ShapeDtypeStruct(total.shape, jnp.float32),
        compiler_params=pltpu.CompilerParams(vmem_limit_bytes=VMEM_LIMIT),
        cost_estimate=pl.CostEstimate(
            flops=8 * y.shape[1] * total.size, bytes_accessed=4 * y.shape[1] * total.shape[1], transcendentals=0
        ),
        name="project_last",
    )(x, y, *kept, total)


def attend(keyed, asked, q_width, kv_width, store):
    groups = kv_width // HEAD_SIZE_DIM
    scale = 1.0 / math.sqrt(HEAD_SIZE_DIM)

    def columns(pairs, start):
        stop = start + HEAD_SIZE_DIM
        return jnp.concatenate([a[:, start:stop] + b[:, start:stop] for a, b in pairs], axis=0)

    rows = sum(a.shape[0] for a, _ in asked)
    together = GROUP if rows <= 64 else 1
    for g in range(groups):
        at = q_width + g * HEAD_SIZE_DIM
        k_high, k_low = split(columns(keyed, at))
        v_high, v_low = split(columns(keyed, at + kv_width))
        k_highs = jnp.concatenate([k_high, k_high], axis=1)
        k_lows = jnp.concatenate([k_low, k_low], axis=1)
        v_both = jnp.concatenate([v_high, v_low], axis=1)
        for j in range(0, GROUP, together):
            heads = [(g * GROUP + j + i) * HEAD_SIZE_DIM for i in range(together)]
            queries = split(jnp.concatenate([columns(asked, h) for h in heads], axis=0) * scale)
            q_both = jnp.concatenate(queries, axis=1)
            scores = dot(q_both, k_highs, ((1,), (1,))) + dot(q_both, k_lows, ((1,), (1,)))
            weights = jnp.exp(scores - jnp.max(scores, axis=-1, keepdims=True))
            total = jnp.sum(weights, axis=-1, keepdims=True)
            p_high, p_low = split(weights)
            both = dot(p_high, v_both)
            less = dot(p_low, v_both)
            result = both[:, :HEAD_SIZE_DIM] + (
                (both[:, HEAD_SIZE_DIM:] + less[:, :HEAD_SIZE_DIM]) + less[:, HEAD_SIZE_DIM:]
            )
            result = result / total
            for i, h in enumerate(heads):
                store(h, result[i * rows : (i + 1) * rows])


def halve_kernel(start, w_ref, before, high, low, buf, sems):
    steps, step, size = buf.shape

    def copy(k):
        return pltpu.make_async_copy(w_ref.at[pl.ds(k * step, step), pl.ds(start, size)], buf.at[k], sems.at[k])

    for k in range(steps):
        copy(k).start()
    for k in range(steps):
        copy(k).wait()
        rows = slice(k * step, (k + 1) * step)
        high[rows], low[rows] = split(buf[k])


def halve(w, start, size, before, step=256):
    steps = w.shape[0] // step
    vmem, anywhere = pl.BlockSpec(memory_space=pltpu.VMEM), pl.BlockSpec(memory_space=pl.ANY)
    return pl.pallas_call(
        functools.partial(halve_kernel, start),
        in_specs=[anywhere] * 2,
        out_specs=[vmem] * 2,
        out_shape=[jax.ShapeDtypeStruct((w.shape[0], size), jnp.bfloat16)] * 2,
        scratch_shapes=[pltpu.VMEM((steps, step, size), jnp.float32), pltpu.SemaphoreType.DMA((steps,))],
        compiler_params=pltpu.CompilerParams(vmem_limit_bytes=VMEM_LIMIT),
        cost_estimate=pl.CostEstimate(flops=w.shape[0] * size, bytes_accessed=8 * w.shape[0] * size, transcendentals=0),
        name="halve",
    )(w, before)


def mix_kernel(n_parts, ask, q_width, kv_width, start, step, is_split, *refs):
    part_refs, rest = refs[:n_parts], refs[n_parts:]
    if is_split:
        (w_high, w_low), outs = rest[:2], rest[2:]
    else:
        w_ref, outs, (buf, sems) = rest[0], rest[1:-2], rest[-2:]

        def copy(k):
            return pltpu.make_async_copy(w_ref.at[:, pl.ds(start + k * step, step)], buf.at[k], sems.at[k])

        for k in range(buf.shape[0]):
            copy(k).start()
    if ask is None:
        high, low = part_refs
    else:
        high, low, outs = outs[0], outs[1], outs[2:]

        def store(head, rows):
            h, l = split(rows)
            high[:, head : head + HEAD_SIZE_DIM] = h
            low[:, head : head + HEAD_SIZE_DIM] = l

        pairs = [(part_refs[2 * i], part_refs[2 * i + 1]) for i in range(n_parts // 2)]
        attend(pairs, pairs[ask], q_width, kv_width, store)
    attended = (high[...], low[...])
    for k in range(outs[0].shape[1] // step):
        columns = slice(k * step, (k + 1) * step)
        if is_split:
            these = slice(start + k * step, start + (k + 1) * step)
            w = (w_high[:, these], w_low[:, these])
        else:
            copy(k).wait()
            w = split(buf[k])
        mixed = dot_split(attended, w)
        at = 0
        for o in outs:
            o[:, columns] = mixed[at : at + o.shape[0]]
            at += o.shape[0]


def mix(operands, ask, rows, keyed, w, kv_width, slots, start, columns, name, step=512):
    q_width, is_split = w[0].shape[0], len(w) == 2
    steps = columns // step
    attended = [jax.ShapeDtypeStruct((rows, q_width), jnp.bfloat16)] * (0 if ask is None else 2)
    out_shape = attended + [jax.ShapeDtypeStruct((s, columns), jnp.float32) for s in slots]
    vmem = pl.BlockSpec(memory_space=pltpu.VMEM)
    scratch = [pltpu.VMEM((steps, q_width, step), jnp.float32), pltpu.SemaphoreType.DMA((steps,))]
    return pl.pallas_call(
        functools.partial(mix_kernel, len(operands), ask, q_width, kv_width, start, step, is_split),
        in_specs=[vmem] * len(operands) + ([vmem] * 2 if is_split else [pl.BlockSpec(memory_space=pl.ANY)]),
        out_specs=[vmem] * len(out_shape),
        out_shape=out_shape,
        scratch_shapes=[] if is_split else scratch,
        compiler_params=pltpu.CompilerParams(vmem_limit_bytes=VMEM_LIMIT),
        cost_estimate=pl.CostEstimate(
            flops=8 * rows * q_width * columns + 32 * rows * keyed * q_width,
            bytes_accessed=4 * columns * (q_width + rows),
            transcendentals=rows * keyed * q_width // HEAD_SIZE_DIM,
        ),
        name=name,
    )(*operands, *w)


def attend_out(parts, first, last, w, kv_width, slots, columns):
    rows = sum(a.shape[0] for a, _ in parts[first:last])
    keyed = sum(a.shape[0] for a, _ in parts)
    flat = [r for pair in parts for r in pair]
    res = mix(flat, slice(first, last), rows, keyed, w, kv_width, slots, 0, columns, "attend_out")
    return res[:2], res[2:]


def out_again(attended, w, slots, start, columns):
    rows = attended[0].shape[0]
    return mix(list(attended), None, rows, 0, w, 0, slots, start, columns, "out_again")


def after(a, *others):
    return lax.optimization_barrier((a, *others))[0]


def cut(sizes):
    return [(sum(sizes[:i]), size) for i, size in enumerate(sizes)]


def on_line_of_four(tokens, w_query, w_key, w_value, w_out):
    rows, depth = tokens.shape
    weights = (w_query, w_key, w_value)
    kv_width = w_key.shape[1]
    halves = cut([depth // 2] * 2)
    last = cut([depth // 2, depth // 4, depth // 4])

    def hop(a, pairs):
        return lax.ppermute(a, "col", pairs)

    def swap(a):
        return lax.ppermute(a, "row", CORES)

    def columns(a, start, size):
        return a[:, start : start + size]

    near = hop(tokens, PAIRS)
    mid = [hop(columns(tokens, *h), MIDDLE) for h in halves]
    first = project([((tokens, 0),)], weights, *halves[0])
    mid[0] = after(mid[0], first)
    end2 = [hop(a, ENDS_IN) for a in mid]
    first = project([((tokens, halves[1][0]),)], weights, *halves[1], first, before=mid[:1])
    near = after(near, first)
    mid2 = [hop(columns(near, *halves[0]), MIDDLE)]
    pieces = cut([w_out.shape[1] // 2] * 2)
    w_split = halve(w_out, *pieces[0], near)
    second = third = None
    for (start, size), m, e in zip(halves, mid, end2):
        block = [((near, start),), ((m, 0), (e, 0))]
        second = project(block, weights, start, size, second, before=[w_split[0], mid[1]])
        if start == 0:
            mid2.append(hop(columns(after(near, w_split[0]), *halves[1]), MIDDLE))
            mid2[0] = after(mid2[0], second)
    first, second = [(a, swap(a)) for a in (first, second)]
    for i, (start, size) in enumerate(last):
        half = start // halves[0][1]
        at = start - halves[half][0]
        far = columns(mid2[half], at, size) if size < halves[0][1] else mid2[half]
        if i == 1:
            far = after(far, second[0])
        end3 = hop(far, ENDS_IN)
        block = ((mid2[half], at), (end3, 0))
        if i == len(last) - 1:
            third = project_last(block, kept, third)
        elif i == len(last) - 2:
            third, *kept = project([block], weights, start, size, third, last[-1][1])
        else:
            third = project([block], weights, start, size, third)
    third = (third, swap(third))

    parts = [first, second, third]
    early = cut([pieces[0][1] // 2] * 2 + [pieces[1][1]])
    a_third, m_third = attend_out(parts, 2, 3, w_split, kv_width, [rows], early[0][1])
    m_third = [m_third[0]] + [
        out_again(a_third, w, [rows], *p)[0] for w, p in zip((w_split, [w_out]), early[1:])
    ]
    r1 = [hop(m, ENDS_OUT) for m in m_third]
    others = [tuple(after(a, r1[0], *m_third) for a in first), second, third]
    a_rest, mixed = attend_out(others, 0, 2, w_split, kv_width, [rows] * 3, pieces[0][1])
    r1[1] = after(r1[1], *a_rest)
    mixed = [mixed, out_again(a_rest, [w_out], [rows] * 3, *pieces[1])]
    far = [jnp.concatenate([m + r for m, r in zip(m_third[:2], r1[:2])], axis=1), m_third[2] + r1[2]]
    result = []
    for (m_own, m_near, m_second), f in zip(mixed, far):
        r2e = hop(m_second, ENDS_OUT)
        r2m = hop(f, MIDDLE)
        r3m = hop(m_second + r2e, MIDDLE)
        r3x = hop(m_near + r2m, PAIRS)
        result.append(m_own + (r3x + r3m))
    return jnp.concatenate(result, axis=1)


def on_device(tokens, w_query, w_key, w_value, w_out):
    highest = lax.Precision.HIGHEST
    gathered = lax.all_gather(tokens, "col", axis=0, tiled=True)
    q_width = w_query.shape[1]
    kv_width = w_key.shape[1]

    def product(weight):
        return jnp.dot(gathered, weight, preferred_element_type=jnp.float32, precision=highest)

    joined = lax.psum_scatter(
        jnp.concatenate([product(w_query), product(w_key), product(w_value)], axis=1),
        "row",
        scatter_dimension=0,
        tiled=True,
    )
    query_rows = joined[:, :q_width]
    keys = lax.all_gather(joined[:, q_width : q_width + kv_width], "row", axis=0, tiled=True)
    values = lax.all_gather(joined[:, q_width + kv_width :], "row", axis=0, tiled=True)
    count_of_rows, count_of_heads = query_rows.shape[0], kv_width // HEAD_SIZE_DIM
    query_rows = query_rows.reshape(count_of_rows, count_of_heads, GROUP, HEAD_SIZE_DIM)
    keys = keys.reshape(-1, count_of_heads, HEAD_SIZE_DIM)
    values = values.reshape(-1, count_of_heads, HEAD_SIZE_DIM)
    scores = jnp.einsum("rkgd,nkd->kgrn", query_rows, keys, precision=highest)
    weights = jax.nn.softmax(scores * (1.0 / math.sqrt(HEAD_SIZE_DIM)), axis=-1)
    attended = jnp.einsum("kgrn,nkd->rkgd", weights, values, precision=highest)
    attended = lax.all_gather(attended.reshape(count_of_rows, q_width), "row", axis=0, tiled=True)
    return lax.psum_scatter(
        jnp.dot(attended, w_out, preferred_element_type=jnp.float32, precision=highest),
        "col",
        scatter_dimension=0,
        tiled=True,
    )


def solution(mesh):
    placed = (
        P(("depth", "col"), "row"),
        P("row", "col"),
        P("row", "col"),
        P("row", "col"),
        P("col", "row"),
    )
    here = mesh.shape["row"] == 2 and mesh.shape["col"] == 4
    return jax.shard_map(
        on_line_of_four if here else on_device,
        mesh=mesh,
        in_specs=placed,
        out_specs=P(("depth", "col"), "row"),
        check_vma=False,
    )
```

```python
import functools
import math

import jax
import jax.numpy as jnp
from jax import lax
from jax.experimental import pallas as pl
from jax.experimental.pallas import tpu as pltpu
from jax.sharding import PartitionSpec as P

QUERY_HEADS = 32
KEY_VALUE_HEADS = 4
HEAD_SIZE_DIM = 128
GROUP = QUERY_HEADS // KEY_VALUE_HEADS

VMEM_LIMIT = 38 * 1024 * 1024

ENDS_IN = [(1, 0), (2, 3)]
ENDS_OUT = [(0, 1), (3, 2)]
PAIRS = [(0, 1), (1, 0), (2, 3), (3, 2)]
MIDDLE = [(1, 2), (2, 1)]
CORES = [(0, 1), (1, 0)]


def split(a):
    high = a.astype(jnp.bfloat16)
    return high, (a - high.astype(jnp.float32)).astype(jnp.bfloat16)


def dot(a, b, dims=((1,), (0,))):
    return lax.dot_general(a, b, (dims, ((), ())), preferred_element_type=jnp.float32)


def dot_split(a, b):
    rows = a[0].shape[0]
    both = jnp.concatenate(a, axis=0)
    high, low = dot(both, b[0]), dot(both, b[1])
    return high[:rows] + ((high[rows:] + low[:rows]) + low[rows:])


def project_kernel(terms, with_total, first, steps, step, keep, n_before, *refs):
    n_x = sum(len(t) for t in terms)
    x_refs, w_refs, rest = refs[:n_x], refs[n_x : n_x + 3], refs[n_x + 3 :]
    total, rest = rest[0], rest[(1 if with_total else 0) + n_before :]
    out, kept, bufs, sems = rest[0], rest[1:-4], rest[-4:-1], rest[-1]

    def copies(k):
        start = first + k * step if k < steps else keep + (k - steps) * step
        rows = pl.ds(start, step)
        return [pltpu.make_async_copy(w.at[rows], b.at[k], sems.at[k, i]) for i, (w, b) in enumerate(zip(w_refs, bufs))]

    for k in range(bufs[0].shape[0]):
        for c in copies(k):
            c.start()
    for k in range(steps):
        blocks, i = [], 0
        for term in terms:
            block = None
            for at in term:
                piece = x_refs[i][:, at + k * step : at + (k + 1) * step]
                block = piece if block is None else block + piece
                i += 1
            blocks.append(block)
        x = split(jnp.concatenate(blocks, axis=0) if len(blocks) > 1 else blocks[0])
        for c in copies(k):
            c.wait()
        offset = 0
        for b in bufs:
            width = b.shape[2]
            columns = slice(offset, offset + width)
            product = dot_split(x, split(b[k]))
            if k > 0:
                out[:, columns] += product
            elif with_total:
                out[:, columns] = total[:, columns] + product
            else:
                out[:, columns] = product
            offset += width
    for k in range(steps, bufs[0].shape[0]):
        for c in copies(k):
            c.wait()
        offset, rows = 0, slice((k - steps) * step, (k - steps + 1) * step)
        for b in bufs:
            columns = slice(offset, offset + b.shape[2])
            kept[0][rows, columns], kept[1][rows, columns] = split(b[k])
            offset += b.shape[2]


def project(blocks, weights, start, depth, total=None, keep=(0, 0), before=(), step=512):
    terms = tuple(tuple(at for _, at in b) for b in blocks)
    operands = [a for b in blocks for a, _ in b]
    rows = sum(b[0][0].shape[0] for b in blocks)
    width = sum(w.shape[1] for w in weights)
    steps = depth // step
    vmem, anywhere = pl.BlockSpec(memory_space=pltpu.VMEM), pl.BlockSpec(memory_space=pl.ANY)
    in_specs = [vmem] * len(operands) + [anywhere] * len(weights)
    operands += weights
    if total is not None:
        in_specs.append(vmem)
        operands.append(total)
    in_specs += [anywhere] * len(before)
    operands += before
    return pl.pallas_call(
        functools.partial(project_kernel, terms, total is not None, start, steps, step, keep[0], len(before)),
        in_specs=in_specs,
        out_specs=[vmem] * 3 if keep[1] else vmem,
        out_shape=[jax.ShapeDtypeStruct((rows, width), jnp.float32)]
        + [jax.ShapeDtypeStruct((keep[1], width), jnp.bfloat16)] * 2
        if keep[1]
        else jax.ShapeDtypeStruct((rows, width), jnp.float32),
        scratch_shapes=[pltpu.VMEM((steps + keep[1] // step, step, w.shape[1]), jnp.float32) for w in weights]
        + [pltpu.SemaphoreType.DMA((steps + keep[1] // step, len(weights)))],
        compiler_params=pltpu.CompilerParams(vmem_limit_bytes=VMEM_LIMIT),
        cost_estimate=pl.CostEstimate(
            flops=8 * rows * depth * width, bytes_accessed=4 * depth * (rows + width), transcendentals=0
        ),
        name="project",
    )(*operands)


def project_last_kernel(at, start, x, y, high, low, total, out):
    size = y.shape[1]
    block = split(x[:, at : at + size] + y[...])
    rows = slice(start, start + size)
    out[...] = total[...] + dot_split(block, (high[rows], low[rows]))


def project_last(block, kept, start, total):
    (x, at), (y, _) = block
    vmem = pl.BlockSpec(memory_space=pltpu.VMEM)
    return pl.pallas_call(
        functools.partial(project_last_kernel, at, start),
        in_specs=[vmem] * 5,
        out_specs=vmem,
        out_shape=jax.ShapeDtypeStruct(total.shape, jnp.float32),
        compiler_params=pltpu.CompilerParams(vmem_limit_bytes=VMEM_LIMIT),
        cost_estimate=pl.CostEstimate(
            flops=8 * y.shape[1] * total.size, bytes_accessed=4 * y.shape[1] * total.shape[1], transcendentals=0
        ),
        name="project_last",
    )(x, y, *kept, total)


def attend(keyed, asked, q_width, kv_width, store):
    groups = kv_width // HEAD_SIZE_DIM
    scale = 1.0 / math.sqrt(HEAD_SIZE_DIM)

    def columns(pairs, start):
        stop = start + HEAD_SIZE_DIM
        return jnp.concatenate([a[:, start:stop] + b[:, start:stop] for a, b in pairs], axis=0)

    rows = sum(a.shape[0] for a, _ in asked)
    together = GROUP if rows <= 64 else 1
    for g in range(groups):
        at = q_width + g * HEAD_SIZE_DIM
        k_high, k_low = split(columns(keyed, at))
        v_high, v_low = split(columns(keyed, at + kv_width))
        k_highs = jnp.concatenate([k_high, k_high], axis=1)
        k_lows = jnp.concatenate([k_low, k_low], axis=1)
        v_both = jnp.concatenate([v_high, v_low], axis=1)
        for j in range(0, GROUP, together):
            heads = [(g * GROUP + j + i) * HEAD_SIZE_DIM for i in range(together)]
            queries = split(jnp.concatenate([columns(asked, h) for h in heads], axis=0) * scale)
            q_both = jnp.concatenate(queries, axis=1)
            scores = dot(q_both, k_highs, ((1,), (1,))) + dot(q_both, k_lows, ((1,), (1,)))
            weights = jnp.exp(scores - jnp.max(scores, axis=-1, keepdims=True))
            total = jnp.sum(weights, axis=-1, keepdims=True)
            p_high, p_low = split(weights)
            both = dot(p_high, v_both)
            less = dot(p_low, v_both)
            result = both[:, :HEAD_SIZE_DIM] + (
                (both[:, HEAD_SIZE_DIM:] + less[:, :HEAD_SIZE_DIM]) + less[:, HEAD_SIZE_DIM:]
            )
            result = result / total
            for i, h in enumerate(heads):
                store(h, result[i * rows : (i + 1) * rows])


def halve_kernel(start, w_ref, before, high, low, buf, sems):
    steps, step, size = buf.shape

    def copy(k):
        return pltpu.make_async_copy(w_ref.at[pl.ds(k * step, step), pl.ds(start, size)], buf.at[k], sems.at[k])

    for k in range(steps):
        copy(k).start()
    for k in range(steps):
        copy(k).wait()
        rows = slice(k * step, (k + 1) * step)
        high[rows], low[rows] = split(buf[k])


def halve(w, start, size, before, step=256):
    steps = w.shape[0] // step
    vmem, anywhere = pl.BlockSpec(memory_space=pltpu.VMEM), pl.BlockSpec(memory_space=pl.ANY)
    return pl.pallas_call(
        functools.partial(halve_kernel, start),
        in_specs=[anywhere] * 2,
        out_specs=[vmem] * 2,
        out_shape=[jax.ShapeDtypeStruct((w.shape[0], size), jnp.bfloat16)] * 2,
        scratch_shapes=[pltpu.VMEM((steps, step, size), jnp.float32), pltpu.SemaphoreType.DMA((steps,))],
        compiler_params=pltpu.CompilerParams(vmem_limit_bytes=VMEM_LIMIT),
        cost_estimate=pl.CostEstimate(flops=w.shape[0] * size, bytes_accessed=8 * w.shape[0] * size, transcendentals=0),
        name="halve",
    )(w, before)


def mix_kernel(n_parts, ask, q_width, kv_width, start, step, is_split, *refs):
    part_refs, rest = refs[:n_parts], refs[n_parts:]
    if is_split:
        (w_high, w_low), outs = rest[:2], rest[2:]
    else:
        w_ref, outs, (buf, sems) = rest[0], rest[1:-2], rest[-2:]

        def copy(k):
            return pltpu.make_async_copy(w_ref.at[:, pl.ds(start + k * step, step)], buf.at[k], sems.at[k])

        for k in range(buf.shape[0]):
            copy(k).start()
    if ask is None:
        high, low = part_refs
    else:
        high, low, outs = outs[0], outs[1], outs[2:]

        def store(head, rows):
            h, l = split(rows)
            high[:, head : head + HEAD_SIZE_DIM] = h
            low[:, head : head + HEAD_SIZE_DIM] = l

        pairs = [(part_refs[2 * i], part_refs[2 * i + 1]) for i in range(n_parts // 2)]
        attend(pairs, pairs[ask], q_width, kv_width, store)
    attended = (high[...], low[...])
    for k in range(outs[0].shape[1] // step):
        columns = slice(k * step, (k + 1) * step)
        if is_split:
            these = slice(start + k * step, start + (k + 1) * step)
            w = (w_high[:, these], w_low[:, these])
        else:
            copy(k).wait()
            w = split(buf[k])
        mixed = dot_split(attended, w)
        at = 0
        for o in outs:
            o[:, columns] = mixed[at : at + o.shape[0]]
            at += o.shape[0]


def mix(operands, ask, rows, keyed, w, kv_width, slots, start, columns, name, step=512):
    q_width, is_split = w[0].shape[0], len(w) == 2
    steps = columns // step
    attended = [jax.ShapeDtypeStruct((rows, q_width), jnp.bfloat16)] * (0 if ask is None else 2)
    out_shape = attended + [jax.ShapeDtypeStruct((s, columns), jnp.float32) for s in slots]
    vmem = pl.BlockSpec(memory_space=pltpu.VMEM)
    scratch = [pltpu.VMEM((steps, q_width, step), jnp.float32), pltpu.SemaphoreType.DMA((steps,))]
    return pl.pallas_call(
        functools.partial(mix_kernel, len(operands), ask, q_width, kv_width, start, step, is_split),
        in_specs=[vmem] * len(operands) + ([vmem] * 2 if is_split else [pl.BlockSpec(memory_space=pl.ANY)]),
        out_specs=[vmem] * len(out_shape),
        out_shape=out_shape,
        scratch_shapes=[] if is_split else scratch,
        compiler_params=pltpu.CompilerParams(vmem_limit_bytes=VMEM_LIMIT),
        cost_estimate=pl.CostEstimate(
            flops=8 * rows * q_width * columns + 32 * rows * keyed * q_width,
            bytes_accessed=4 * columns * (q_width + rows),
            transcendentals=rows * keyed * q_width // HEAD_SIZE_DIM,
        ),
        name=name,
    )(*operands, *w)


def attend_out(parts, first, last, w, kv_width, slots, columns):
    rows = sum(a.shape[0] for a, _ in parts[first:last])
    keyed = sum(a.shape[0] for a, _ in parts)
    flat = [r for pair in parts for r in pair]
    res = mix(flat, slice(first, last), rows, keyed, w, kv_width, slots, 0, columns, "attend_out")
    return res[:2], res[2:]


def out_again(attended, w, slots, start, columns):
    rows = attended[0].shape[0]
    return mix(list(attended), None, rows, 0, w, 0, slots, start, columns, "out_again")


def after(a, *others):
    return lax.optimization_barrier((a, *others))[0]


def cut(sizes):
    return [(sum(sizes[:i]), size) for i, size in enumerate(sizes)]


def on_line_of_four(tokens, w_query, w_key, w_value, w_out):
    rows, depth = tokens.shape
    weights = (w_query, w_key, w_value)
    kv_width = w_key.shape[1]
    halves = cut([depth // 2] * 2)
    last = cut([depth // 2, depth // 4, depth // 4])
    later = (3 * depth // 4, depth // 4)

    def hop(a, pairs):
        return lax.ppermute(a, "col", pairs)

    def swap(a):
        return lax.ppermute(a, "row", CORES)

    def columns(a, start, size):
        return a[:, start : start + size]

    near = hop(tokens, PAIRS)
    mid = [hop(columns(tokens, *h), MIDDLE) for h in halves]
    first = project([((tokens, 0),)], weights, *halves[0])
    mid[0] = after(mid[0], first)
    end2 = [hop(a, ENDS_IN) for a in mid]
    first = project([((tokens, halves[1][0]),)], weights, *halves[1], first, before=mid[:1])
    near = after(near, first)
    mid2 = [hop(columns(near, *halves[0]), MIDDLE)]
    pieces = cut([w_out.shape[1] // 2] * 2)
    w_split = halve(w_out, *pieces[0], near)
    second = third = None
    for (start, size), m, e in zip(halves, mid, end2):
        block = [((near, start),), ((m, 0), (e, 0))]
        second = project(block, weights, start, size, second, before=[w_split[0], mid[1]])
        if start == 0:
            mid2.append(hop(columns(after(near, w_split[0]), *halves[1]), MIDDLE))
            mid2[0] = after(mid2[0], second)
    first, second = [(a, swap(a)) for a in (first, second)]
    for i, (start, size) in enumerate(last):
        half = start // halves[0][1]
        at = start - halves[half][0]
        far = columns(mid2[half], at, size) if size < halves[0][1] else mid2[half]
        if i == 1:
            far = after(far, second[0])
        end3 = hop(far, ENDS_IN)
        block = ((mid2[half], at), (end3, 0))
        if i > 1:
            third = project_last(block, kept, start - later[0], third)
        elif i == 1:
            third = project([block], weights, start, size, third)
        else:
            third, *kept = project([block], weights, start, size, third, later)
    third = (third, swap(third))

    parts = [first, second, third]
    early = cut([pieces[0][1] // 4] * 2 + [pieces[0][1] // 2, pieces[1][1]])
    a_third, m_third = attend_out(parts, 2, 3, w_split, kv_width, [rows], early[0][1])
    m_third = [m_third[0]] + [
        out_again(a_third, w, [rows], *p)[0] for w, p in zip((w_split, w_split, [w_out]), early[1:])
    ]
    r1 = [hop(m, ENDS_OUT) for m in m_third]
    others = [tuple(after(a, r1[0], *m_third) for a in first), second, third]
    a_rest, mixed = attend_out(others, 0, 2, w_split, kv_width, [rows] * 3, pieces[0][1])
    r1[1:3] = [after(r, *a_rest) for r in r1[1:3]]
    mixed = [mixed, out_again(a_rest, [w_out], [rows] * 3, *pieces[1])]
    far = [jnp.concatenate([m + r for m, r in zip(m_third[:3], r1[:3])], axis=1), m_third[3] + r1[3]]
    result = []
    for (m_own, m_near, m_second), f in zip(mixed, far):
        r2e = hop(m_second, ENDS_OUT)
        r2m = hop(f, MIDDLE)
        r3m = hop(m_second + r2e, MIDDLE)
        r3x = hop(m_near + r2m, PAIRS)
        result.append(m_own + (r3x + r3m))
    return jnp.concatenate(result, axis=1)


def on_device(tokens, w_query, w_key, w_value, w_out):
    highest = lax.Precision.HIGHEST
    gathered = lax.all_gather(tokens, "col", axis=0, tiled=True)
    q_width = w_query.shape[1]
    kv_width = w_key.shape[1]

    def product(weight):
        return jnp.dot(gathered, weight, preferred_element_type=jnp.float32, precision=highest)

    joined = lax.psum_scatter(
        jnp.concatenate([product(w_query), product(w_key), product(w_value)], axis=1),
        "row",
        scatter_dimension=0,
        tiled=True,
    )
    query_rows = joined[:, :q_width]
    keys = lax.all_gather(joined[:, q_width : q_width + kv_width], "row", axis=0, tiled=True)
    values = lax.all_gather(joined[:, q_width + kv_width :], "row", axis=0, tiled=True)
    count_of_rows, count_of_heads = query_rows.shape[0], kv_width // HEAD_SIZE_DIM
    query_rows = query_rows.reshape(count_of_rows, count_of_heads, GROUP, HEAD_SIZE_DIM)
    keys = keys.reshape(-1, count_of_heads, HEAD_SIZE_DIM)
    values = values.reshape(-1, count_of_heads, HEAD_SIZE_DIM)
    scores = jnp.einsum("rkgd,nkd->kgrn", query_rows, keys, precision=highest)
    weights = jax.nn.softmax(scores * (1.0 / math.sqrt(HEAD_SIZE_DIM)), axis=-1)
    attended = jnp.einsum("kgrn,nkd->rkgd", weights, values, precision=highest)
    attended = lax.all_gather(attended.reshape(count_of_rows, q_width), "row", axis=0, tiled=True)
    return lax.psum_scatter(
        jnp.dot(attended, w_out, preferred_element_type=jnp.float32, precision=highest),
        "col",
        scatter_dimension=0,
        tiled=True,
    )


def solution(mesh):
    placed = (
        P(("depth", "col"), "row"),
        P("row", "col"),
        P("row", "col"),
        P("row", "col"),
        P("col", "row"),
    )
    here = mesh.shape["row"] == 2 and mesh.shape["col"] == 4
    return jax.shard_map(
        on_line_of_four if here else on_device,
        mesh=mesh,
        in_specs=placed,
        out_specs=P(("depth", "col"), "row"),
        check_vma=False,
    )
```

```python
import functools
import math

import jax
import jax.numpy as jnp
from jax import lax
from jax.experimental import pallas as pl
from jax.experimental.pallas import tpu as pltpu
from jax.sharding import PartitionSpec as P

QUERY_HEADS = 32
KEY_VALUE_HEADS = 4
HEAD_SIZE_DIM = 128
GROUP = QUERY_HEADS // KEY_VALUE_HEADS

VMEM_LIMIT = 38 * 1024 * 1024

ENDS_IN = [(1, 0), (2, 3)]
ENDS_OUT = [(0, 1), (3, 2)]
PAIRS = [(0, 1), (1, 0), (2, 3), (3, 2)]
MIDDLE = [(1, 2), (2, 1)]
CORES = [(0, 1), (1, 0)]


def split(a):
    high = a.astype(jnp.bfloat16)
    return high, (a - high.astype(jnp.float32)).astype(jnp.bfloat16)


def dot(a, b, dims=((1,), (0,))):
    return lax.dot_general(a, b, (dims, ((), ())), preferred_element_type=jnp.float32)


def dot_split(a, b):
    rows = a[0].shape[0]
    both = jnp.concatenate(a, axis=0)
    high, low = dot(both, b[0]), dot(both, b[1])
    return high[:rows] + ((high[rows:] + low[:rows]) + low[rows:])


def project_kernel(terms, with_total, first, steps, step, keep, n_before, *refs):
    n_x = sum(len(t) for t in terms)
    x_refs, w_refs, rest = refs[:n_x], refs[n_x : n_x + 3], refs[n_x + 3 :]
    total, rest = rest[0], rest[(1 if with_total else 0) + n_before :]
    out, kept, bufs, sems = rest[0], rest[1:-4], rest[-4:-1], rest[-1]

    def copies(k):
        start = first + k * step if k < steps else keep + (k - steps) * step
        rows = pl.ds(start, step)
        return [pltpu.make_async_copy(w.at[rows], b.at[k], sems.at[k, i]) for i, (w, b) in enumerate(zip(w_refs, bufs))]

    for k in range(bufs[0].shape[0]):
        for c in copies(k):
            c.start()
    for k in range(steps):
        blocks, i = [], 0
        for term in terms:
            block = None
            for at in term:
                piece = x_refs[i][:, at + k * step : at + (k + 1) * step]
                block = piece if block is None else block + piece
                i += 1
            blocks.append(block)
        x = split(jnp.concatenate(blocks, axis=0) if len(blocks) > 1 else blocks[0])
        for c in copies(k):
            c.wait()
        offset = 0
        for b in bufs:
            width = b.shape[2]
            columns = slice(offset, offset + width)
            product = dot_split(x, split(b[k]))
            if k > 0:
                out[:, columns] += product
            elif with_total:
                out[:, columns] = total[:, columns] + product
            else:
                out[:, columns] = product
            offset += width
    for k in range(steps, bufs[0].shape[0]):
        for c in copies(k):
            c.wait()
        offset, rows = 0, slice((k - steps) * step, (k - steps + 1) * step)
        for b in bufs:
            columns = slice(offset, offset + b.shape[2])
            kept[0][rows, columns], kept[1][rows, columns] = split(b[k])
            offset += b.shape[2]


def project(blocks, weights, start, depth, total=None, keep=(0, 0), before=(), step=512):
    terms = tuple(tuple(at for _, at in b) for b in blocks)
    operands = [a for b in blocks for a, _ in b]
    rows = sum(b[0][0].shape[0] for b in blocks)
    width = sum(w.shape[1] for w in weights)
    steps = depth // step
    vmem, anywhere = pl.BlockSpec(memory_space=pltpu.VMEM), pl.BlockSpec(memory_space=pl.ANY)
    in_specs = [vmem] * len(operands) + [anywhere] * len(weights)
    operands += weights
    if total is not None:
        in_specs.append(vmem)
        operands.append(total)
    in_specs += [anywhere] * len(before)
    operands += before
    return pl.pallas_call(
        functools.partial(project_kernel, terms, total is not None, start, steps, step, keep[0], len(before)),
        in_specs=in_specs,
        out_specs=[vmem] * 3 if keep[1] else vmem,
        out_shape=[jax.ShapeDtypeStruct((rows, width), jnp.float32)]
        + [jax.ShapeDtypeStruct((keep[1], width), jnp.bfloat16)] * 2
        if keep[1]
        else jax.ShapeDtypeStruct((rows, width), jnp.float32),
        scratch_shapes=[pltpu.VMEM((steps + keep[1] // step, step, w.shape[1]), jnp.float32) for w in weights]
        + [pltpu.SemaphoreType.DMA((steps + keep[1] // step, len(weights)))],
        compiler_params=pltpu.CompilerParams(vmem_limit_bytes=VMEM_LIMIT),
        cost_estimate=pl.CostEstimate(
            flops=8 * rows * depth * width, bytes_accessed=4 * depth * (rows + width), transcendentals=0
        ),
        name="project",
    )(*operands)


def project_last_kernel(at, start, x, y, high, low, total, out):
    size = y.shape[1]
    block = split(x[:, at : at + size] + y[...])
    rows = slice(start, start + size)
    out[...] = total[...] + dot_split(block, (high[rows], low[rows]))


def project_last(block, kept, start, total):
    (x, at), (y, _) = block
    vmem = pl.BlockSpec(memory_space=pltpu.VMEM)
    return pl.pallas_call(
        functools.partial(project_last_kernel, at, start),
        in_specs=[vmem] * 5,
        out_specs=vmem,
        out_shape=jax.ShapeDtypeStruct(total.shape, jnp.float32),
        compiler_params=pltpu.CompilerParams(vmem_limit_bytes=VMEM_LIMIT),
        cost_estimate=pl.CostEstimate(
            flops=8 * y.shape[1] * total.size, bytes_accessed=4 * y.shape[1] * total.shape[1], transcendentals=0
        ),
        name="project_last",
    )(x, y, *kept, total)


def attend(keyed, asked, q_width, kv_width, store):
    groups = kv_width // HEAD_SIZE_DIM
    scale = 1.0 / math.sqrt(HEAD_SIZE_DIM)

    def columns(pairs, start):
        stop = start + HEAD_SIZE_DIM
        return jnp.concatenate([a[:, start:stop] + b[:, start:stop] for a, b in pairs], axis=0)

    rows = sum(a.shape[0] for a, _ in asked)
    together = GROUP if rows <= 64 else 1
    for g in range(groups):
        at = q_width + g * HEAD_SIZE_DIM
        k_high, k_low = split(columns(keyed, at))
        v_high, v_low = split(columns(keyed, at + kv_width))
        k_highs = jnp.concatenate([k_high, k_high], axis=1)
        k_lows = jnp.concatenate([k_low, k_low], axis=1)
        v_both = jnp.concatenate([v_high, v_low], axis=1)
        for j in range(0, GROUP, together):
            heads = [(g * GROUP + j + i) * HEAD_SIZE_DIM for i in range(together)]
            queries = split(jnp.concatenate([columns(asked, h) for h in heads], axis=0) * scale)
            q_both = jnp.concatenate(queries, axis=1)
            scores = dot(q_both, k_highs, ((1,), (1,))) + dot(q_both, k_lows, ((1,), (1,)))
            weights = jnp.exp(scores - jnp.max(scores, axis=-1, keepdims=True))
            total = jnp.sum(weights, axis=-1, keepdims=True)
            p_high, p_low = split(weights)
            both = dot(p_high, v_both)
            less = dot(p_low, v_both)
            result = both[:, :HEAD_SIZE_DIM] + (
                (both[:, HEAD_SIZE_DIM:] + less[:, :HEAD_SIZE_DIM]) + less[:, HEAD_SIZE_DIM:]
            )
            result = result / total
            for i, h in enumerate(heads):
                store(h, result[i * rows : (i + 1) * rows])


def halve_kernel(start, w_ref, before, high, low, buf, sems):
    steps, step, size = buf.shape

    def copy(k):
        return pltpu.make_async_copy(w_ref.at[pl.ds(k * step, step), pl.ds(start, size)], buf.at[k], sems.at[k])

    for k in range(steps):
        copy(k).start()
    for k in range(steps):
        copy(k).wait()
        rows = slice(k * step, (k + 1) * step)
        high[rows], low[rows] = split(buf[k])


def halve(w, start, size, before, step=256):
    steps = w.shape[0] // step
    vmem, anywhere = pl.BlockSpec(memory_space=pltpu.VMEM), pl.BlockSpec(memory_space=pl.ANY)
    return pl.pallas_call(
        functools.partial(halve_kernel, start),
        in_specs=[anywhere] * 2,
        out_specs=[vmem] * 2,
        out_shape=[jax.ShapeDtypeStruct((w.shape[0], size), jnp.bfloat16)] * 2,
        scratch_shapes=[pltpu.VMEM((steps, step, size), jnp.float32), pltpu.SemaphoreType.DMA((steps,))],
        compiler_params=pltpu.CompilerParams(vmem_limit_bytes=VMEM_LIMIT),
        cost_estimate=pl.CostEstimate(flops=w.shape[0] * size, bytes_accessed=8 * w.shape[0] * size, transcendentals=0),
        name="halve",
    )(w, before)


def mix_kernel(n_parts, ask, q_width, kv_width, start, step, is_split, *refs):
    part_refs, rest = refs[:n_parts], refs[n_parts:]
    if is_split:
        (w_high, w_low), outs = rest[:2], rest[2:]
    else:
        w_ref, outs, (buf, sems) = rest[0], rest[1:-2], rest[-2:]

        def copy(k):
            return pltpu.make_async_copy(w_ref.at[:, pl.ds(start + k * step, step)], buf.at[k], sems.at[k])

        for k in range(buf.shape[0]):
            copy(k).start()
    if ask is None:
        high, low = part_refs
    else:
        high, low, outs = outs[0], outs[1], outs[2:]

        def store(head, rows):
            h, l = split(rows)
            high[:, head : head + HEAD_SIZE_DIM] = h
            low[:, head : head + HEAD_SIZE_DIM] = l

        pairs = [(part_refs[2 * i], part_refs[2 * i + 1]) for i in range(n_parts // 2)]
        attend(pairs, pairs[ask], q_width, kv_width, store)
    attended = (high[...], low[...])
    for k in range(outs[0].shape[1] // step):
        columns = slice(k * step, (k + 1) * step)
        if is_split:
            these = slice(start + k * step, start + (k + 1) * step)
            w = (w_high[:, these], w_low[:, these])
        else:
            copy(k).wait()
            w = split(buf[k])
        mixed = dot_split(attended, w)
        at = 0
        for o in outs:
            o[:, columns] = mixed[at : at + o.shape[0]]
            at += o.shape[0]


def mix(operands, ask, rows, keyed, w, kv_width, slots, start, columns, name, step=512):
    q_width, is_split = w[0].shape[0], len(w) == 2
    steps = columns // step
    attended = [jax.ShapeDtypeStruct((rows, q_width), jnp.bfloat16)] * (0 if ask is None else 2)
    out_shape = attended + [jax.ShapeDtypeStruct((s, columns), jnp.float32) for s in slots]
    vmem = pl.BlockSpec(memory_space=pltpu.VMEM)
    scratch = [pltpu.VMEM((steps, q_width, step), jnp.float32), pltpu.SemaphoreType.DMA((steps,))]
    return pl.pallas_call(
        functools.partial(mix_kernel, len(operands), ask, q_width, kv_width, start, step, is_split),
        in_specs=[vmem] * len(operands) + ([vmem] * 2 if is_split else [pl.BlockSpec(memory_space=pl.ANY)]),
        out_specs=[vmem] * len(out_shape),
        out_shape=out_shape,
        scratch_shapes=[] if is_split else scratch,
        compiler_params=pltpu.CompilerParams(vmem_limit_bytes=VMEM_LIMIT),
        cost_estimate=pl.CostEstimate(
            flops=8 * rows * q_width * columns + 32 * rows * keyed * q_width,
            bytes_accessed=4 * columns * (q_width + rows),
            transcendentals=rows * keyed * q_width // HEAD_SIZE_DIM,
        ),
        name=name,
    )(*operands, *w)


def attend_out(parts, first, last, w, kv_width, slots, columns):
    rows = sum(a.shape[0] for a, _ in parts[first:last])
    keyed = sum(a.shape[0] for a, _ in parts)
    flat = [r for pair in parts for r in pair]
    res = mix(flat, slice(first, last), rows, keyed, w, kv_width, slots, 0, columns, "attend_out")
    return res[:2], res[2:]


def out_again(attended, w, slots, start, columns):
    rows = attended[0].shape[0]
    return mix(list(attended), None, rows, 0, w, 0, slots, start, columns, "out_again")


def after(a, *others):
    return lax.optimization_barrier((a, *others))[0]


def cut(sizes):
    return [(sum(sizes[:i]), size) for i, size in enumerate(sizes)]


def on_line_of_four(tokens, w_query, w_key, w_value, w_out):
    rows, depth = tokens.shape
    weights = (w_query, w_key, w_value)
    kv_width = w_key.shape[1]
    halves = cut([depth // 2] * 2)
    last = cut([depth // 2, depth // 4, depth // 4])
    later = (3 * depth // 4, depth // 4)

    def hop(a, pairs):
        return lax.ppermute(a, "col", pairs)

    def swap(a):
        return lax.ppermute(a, "row", CORES)

    def columns(a, start, size):
        return a[:, start : start + size]

    near = hop(tokens, PAIRS)
    mid = [hop(columns(tokens, *h), MIDDLE) for h in halves]
    first = project([((tokens, 0),)], weights, *halves[0])
    mid[0] = after(mid[0], first)
    end2 = [hop(a, ENDS_IN) for a in mid]
    first = project([((tokens, halves[1][0]),)], weights, *halves[1], first, before=mid[:1])
    near = after(near, first)
    mid2 = [hop(columns(near, *halves[0]), MIDDLE)]
    pieces = cut([w_out.shape[1] // 2] * 2)
    w_split = halve(w_out, *pieces[0], near)
    second = third = None
    for (start, size), m, e in zip(halves, mid, end2):
        block = [((near, start),), ((m, 0), (e, 0))]
        second = project(block, weights, start, size, second, before=[w_split[0], mid[1]])
        if start == 0:
            mid2.append(hop(columns(after(near, w_split[0]), *halves[1]), MIDDLE))
            mid2[0] = after(mid2[0], second)
    first, second = [(a, swap(a)) for a in (first, second)]
    for i, (start, size) in enumerate(last):
        half = start // halves[0][1]
        at = start - halves[half][0]
        far = columns(mid2[half], at, size) if size < halves[0][1] else mid2[half]
        if i == 1:
            far = after(far, second[0])
        end3 = hop(far, ENDS_IN)
        block = ((mid2[half], at), (end3, 0))
        if i > 1:
            third = project_last(block, kept, start - later[0], third)
        elif i == 1:
            third = project([block], weights, start, size, third)
        else:
            third, *kept = project([block], weights, start, size, third, later)
    third = (third, swap(third))

    parts = [first, second, third]
    early = cut([pieces[0][1] // 4] * 2 + [pieces[0][1] // 2, pieces[1][1]])
    a_third, m_third = attend_out(parts, 2, 3, w_split, kv_width, [rows], early[0][1])
    m_third = [m_third[0]] + [
        out_again(a_third, w, [rows], *p)[0] for w, p in zip((w_split, w_split, [w_out]), early[1:])
    ]
    r1 = [hop(m, ENDS_OUT) for m in m_third]
    others = [tuple(after(a, r1[0], *m_third) for a in first), second, third]
    a_rest, mixed = attend_out(others, 0, 2, w_split, kv_width, [rows] * 3, pieces[0][1])
    r1[1:3] = [after(r, *a_rest) for r in r1[1:3]]
    mixed = [mixed, out_again(a_rest, [w_out], [rows] * 3, *pieces[1])]
    far = [jnp.concatenate([m + r for m, r in zip(m_third[:3], r1[:3])], axis=1), m_third[3] + r1[3]]
    result = []
    for (m_own, m_near, m_second), f in zip(mixed, far):
        r2e = hop(m_second, ENDS_OUT)
        r2m = hop(f, MIDDLE)
        r3m = hop(m_second + r2e, MIDDLE)
        r3x = hop(m_near + r2m, PAIRS)
        result.append(m_own + (r3x + r3m))
    size = pieces[0][1]
    left = jnp.pad(result[0], ((0, 0), (0, size)))
    return left + jnp.pad(result[1], ((0, 0), (size, 0)))


def on_device(tokens, w_query, w_key, w_value, w_out):
    highest = lax.Precision.HIGHEST
    gathered = lax.all_gather(tokens, "col", axis=0, tiled=True)
    q_width = w_query.shape[1]
    kv_width = w_key.shape[1]

    def product(weight):
        return jnp.dot(gathered, weight, preferred_element_type=jnp.float32, precision=highest)

    joined = lax.psum_scatter(
        jnp.concatenate([product(w_query), product(w_key), product(w_value)], axis=1),
        "row",
        scatter_dimension=0,
        tiled=True,
    )
    query_rows = joined[:, :q_width]
    keys = lax.all_gather(joined[:, q_width : q_width + kv_width], "row", axis=0, tiled=True)
    values = lax.all_gather(joined[:, q_width + kv_width :], "row", axis=0, tiled=True)
    count_of_rows, count_of_heads = query_rows.shape[0], kv_width // HEAD_SIZE_DIM
    query_rows = query_rows.reshape(count_of_rows, count_of_heads, GROUP, HEAD_SIZE_DIM)
    keys = keys.reshape(-1, count_of_heads, HEAD_SIZE_DIM)
    values = values.reshape(-1, count_of_heads, HEAD_SIZE_DIM)
    scores = jnp.einsum("rkgd,nkd->kgrn", query_rows, keys, precision=highest)
    weights = jax.nn.softmax(scores * (1.0 / math.sqrt(HEAD_SIZE_DIM)), axis=-1)
    attended = jnp.einsum("kgrn,nkd->rkgd", weights, values, precision=highest)
    attended = lax.all_gather(attended.reshape(count_of_rows, q_width), "row", axis=0, tiled=True)
    return lax.psum_scatter(
        jnp.dot(attended, w_out, preferred_element_type=jnp.float32, precision=highest),
        "col",
        scatter_dimension=0,
        tiled=True,
    )


def solution(mesh):
    placed = (
        P(("depth", "col"), "row"),
        P("row", "col"),
        P("row", "col"),
        P("row", "col"),
        P("col", "row"),
    )
    here = mesh.shape["row"] == 2 and mesh.shape["col"] == 4
    return jax.shard_map(
        on_line_of_four if here else on_device,
        mesh=mesh,
        in_specs=placed,
        out_specs=P(("depth", "col"), "row"),
        check_vma=False,
    )
```

```python
import functools
import math

import jax
import jax.numpy as jnp
from jax import lax
from jax.experimental import pallas as pl
from jax.experimental.pallas import tpu as pltpu
from jax.sharding import PartitionSpec as P

QUERY_HEADS = 32
KEY_VALUE_HEADS = 4
HEAD_SIZE_DIM = 128
GROUP = QUERY_HEADS // KEY_VALUE_HEADS

VMEM_LIMIT = 38 * 1024 * 1024

ENDS_IN = [(1, 0), (2, 3)]
ENDS_OUT = [(0, 1), (3, 2)]
PAIRS = [(0, 1), (1, 0), (2, 3), (3, 2)]
MIDDLE = [(1, 2), (2, 1)]
CORES = [(0, 1), (1, 0)]


def split(a):
    high = a.astype(jnp.bfloat16)
    return high, (a - high.astype(jnp.float32)).astype(jnp.bfloat16)


def dot(a, b, dims=((1,), (0,))):
    return lax.dot_general(a, b, (dims, ((), ())), preferred_element_type=jnp.float32)


def dot_split(a, b):
    rows = a[0].shape[0]
    both = jnp.concatenate(a, axis=0)
    high, low = dot(both, b[0]), dot(both, b[1])
    return high[:rows] + ((high[rows:] + low[:rows]) + low[rows:])


def project_kernel(terms, with_total, first, steps, step, keep, n_before, *refs):
    n_x = sum(len(t) for t in terms)
    x_refs, w_refs, rest = refs[:n_x], refs[n_x : n_x + 3], refs[n_x + 3 :]
    total, rest = rest[0], rest[(1 if with_total else 0) + n_before :]
    out, kept, bufs, sems = rest[0], rest[1:-4], rest[-4:-1], rest[-1]

    def copies(k):
        start = first + k * step if k < steps else keep + (k - steps) * step
        rows = pl.ds(start, step)
        return [pltpu.make_async_copy(w.at[rows], b.at[k], sems.at[k, i]) for i, (w, b) in enumerate(zip(w_refs, bufs))]

    for k in range(bufs[0].shape[0]):
        for c in copies(k):
            c.start()
    for k in range(steps):
        blocks, i = [], 0
        for term in terms:
            block = None
            for at in term:
                piece = x_refs[i][:, at + k * step : at + (k + 1) * step]
                block = piece if block is None else block + piece
                i += 1
            blocks.append(block)
        x = split(jnp.concatenate(blocks, axis=0) if len(blocks) > 1 else blocks[0])
        for c in copies(k):
            c.wait()
        offset = 0
        for b in bufs:
            width = b.shape[2]
            columns = slice(offset, offset + width)
            product = dot_split(x, split(b[k]))
            if k > 0:
                out[:, columns] += product
            elif with_total:
                out[:, columns] = total[:, columns] + product
            else:
                out[:, columns] = product
            offset += width
    for k in range(steps, bufs[0].shape[0]):
        for c in copies(k):
            c.wait()
        offset, rows = 0, slice((k - steps) * step, (k - steps + 1) * step)
        for b in bufs:
            columns = slice(offset, offset + b.shape[2])
            kept[0][rows, columns], kept[1][rows, columns] = split(b[k])
            offset += b.shape[2]


def project(blocks, weights, start, depth, total=None, keep=(0, 0), before=(), step=512):
    terms = tuple(tuple(at for _, at in b) for b in blocks)
    operands = [a for b in blocks for a, _ in b]
    rows = sum(b[0][0].shape[0] for b in blocks)
    width = sum(w.shape[1] for w in weights)
    steps = depth // step
    vmem, anywhere = pl.BlockSpec(memory_space=pltpu.VMEM), pl.BlockSpec(memory_space=pl.ANY)
    in_specs = [vmem] * len(operands) + [anywhere] * len(weights)
    operands += weights
    if total is not None:
        in_specs.append(vmem)
        operands.append(total)
    in_specs += [anywhere] * len(before)
    operands += before
    return pl.pallas_call(
        functools.partial(project_kernel, terms, total is not None, start, steps, step, keep[0], len(before)),
        in_specs=in_specs,
        out_specs=[vmem] * 3 if keep[1] else vmem,
        out_shape=[jax.ShapeDtypeStruct((rows, width), jnp.float32)]
        + [jax.ShapeDtypeStruct((keep[1], width), jnp.bfloat16)] * 2
        if keep[1]
        else jax.ShapeDtypeStruct((rows, width), jnp.float32),
        scratch_shapes=[pltpu.VMEM((steps + keep[1] // step, step, w.shape[1]), jnp.float32) for w in weights]
        + [pltpu.SemaphoreType.DMA((steps + keep[1] // step, len(weights)))],
        compiler_params=pltpu.CompilerParams(vmem_limit_bytes=VMEM_LIMIT),
        cost_estimate=pl.CostEstimate(
            flops=8 * rows * depth * width, bytes_accessed=4 * depth * (rows + width), transcendentals=0
        ),
        name="project",
    )(*operands)


def project_last_kernel(at, start, x, y, high, low, total, out):
    size = y.shape[1]
    block = split(x[:, at : at + size] + y[...])
    rows = slice(start, start + size)
    out[...] = total[...] + dot_split(block, (high[rows], low[rows]))


def project_last(block, kept, start, total):
    (x, at), (y, _) = block
    vmem = pl.BlockSpec(memory_space=pltpu.VMEM)
    return pl.pallas_call(
        functools.partial(project_last_kernel, at, start),
        in_specs=[vmem] * 5,
        out_specs=vmem,
        out_shape=jax.ShapeDtypeStruct(total.shape, jnp.float32),
        compiler_params=pltpu.CompilerParams(vmem_limit_bytes=VMEM_LIMIT),
        cost_estimate=pl.CostEstimate(
            flops=8 * y.shape[1] * total.size, bytes_accessed=4 * y.shape[1] * total.shape[1], transcendentals=0
        ),
        name="project_last",
    )(x, y, *kept, total)


def attend(keyed, asked, q_width, kv_width, store):
    groups = kv_width // HEAD_SIZE_DIM
    scale = 1.0 / math.sqrt(HEAD_SIZE_DIM)

    def columns(pairs, start):
        stop = start + HEAD_SIZE_DIM
        return jnp.concatenate([a[:, start:stop] + b[:, start:stop] for a, b in pairs], axis=0)

    rows = sum(a.shape[0] for a, _ in asked)
    together = GROUP if rows <= 64 else 1
    for g in range(groups):
        at = q_width + g * HEAD_SIZE_DIM
        k_high, k_low = split(columns(keyed, at))
        v_high, v_low = split(columns(keyed, at + kv_width))
        k_highs = jnp.concatenate([k_high, k_high], axis=1)
        k_lows = jnp.concatenate([k_low, k_low], axis=1)
        v_both = jnp.concatenate([v_high, v_low], axis=1)
        for j in range(0, GROUP, together):
            heads = [(g * GROUP + j + i) * HEAD_SIZE_DIM for i in range(together)]
            queries = split(jnp.concatenate([columns(asked, h) for h in heads], axis=0) * scale)
            q_both = jnp.concatenate(queries, axis=1)
            scores = dot(q_both, k_highs, ((1,), (1,))) + dot(q_both, k_lows, ((1,), (1,)))
            weights = jnp.exp(scores - jnp.max(scores, axis=-1, keepdims=True))
            total = jnp.sum(weights, axis=-1, keepdims=True)
            p_high, p_low = split(weights)
            both = dot(p_high, v_both)
            less = dot(p_low, v_both)
            result = both[:, :HEAD_SIZE_DIM] + (
                (both[:, HEAD_SIZE_DIM:] + less[:, :HEAD_SIZE_DIM]) + less[:, HEAD_SIZE_DIM:]
            )
            result = result / total
            for i, h in enumerate(heads):
                store(h, result[i * rows : (i + 1) * rows])


def halve_kernel(start, w_ref, before, high, low, buf, sems):
    steps, step, size = buf.shape

    def copy(k):
        return pltpu.make_async_copy(w_ref.at[pl.ds(k * step, step), pl.ds(start, size)], buf.at[k], sems.at[k])

    for k in range(steps):
        copy(k).start()
    for k in range(steps):
        copy(k).wait()
        rows = slice(k * step, (k + 1) * step)
        high[rows], low[rows] = split(buf[k])


def halve(w, start, size, before, step=256):
    steps = w.shape[0] // step
    vmem, anywhere = pl.BlockSpec(memory_space=pltpu.VMEM), pl.BlockSpec(memory_space=pl.ANY)
    return pl.pallas_call(
        functools.partial(halve_kernel, start),
        in_specs=[anywhere] * 2,
        out_specs=[vmem] * 2,
        out_shape=[jax.ShapeDtypeStruct((w.shape[0], size), jnp.bfloat16)] * 2,
        scratch_shapes=[pltpu.VMEM((steps, step, size), jnp.float32), pltpu.SemaphoreType.DMA((steps,))],
        compiler_params=pltpu.CompilerParams(vmem_limit_bytes=VMEM_LIMIT),
        cost_estimate=pl.CostEstimate(flops=w.shape[0] * size, bytes_accessed=8 * w.shape[0] * size, transcendentals=0),
        name="halve",
    )(w, before)


def mix_kernel(n_parts, ask, q_width, kv_width, start, step, is_split, *refs):
    part_refs, rest = refs[:n_parts], refs[n_parts:]
    if is_split:
        (w_high, w_low), outs = rest[:2], rest[2:]
    else:
        w_ref, outs, (buf, sems) = rest[0], rest[1:-2], rest[-2:]

        def copy(k):
            return pltpu.make_async_copy(w_ref.at[:, pl.ds(start + k * step, step)], buf.at[k], sems.at[k])

        for k in range(buf.shape[0]):
            copy(k).start()
    if ask is None:
        high, low = part_refs
    else:
        high, low, outs = outs[0], outs[1], outs[2:]

        def store(head, rows):
            h, l = split(rows)
            high[:, head : head + HEAD_SIZE_DIM] = h
            low[:, head : head + HEAD_SIZE_DIM] = l

        pairs = [(part_refs[2 * i], part_refs[2 * i + 1]) for i in range(n_parts // 2)]
        attend(pairs, pairs[ask], q_width, kv_width, store)
    attended = (high[...], low[...])
    for k in range(outs[0].shape[1] // step):
        columns = slice(k * step, (k + 1) * step)
        if is_split:
            these = slice(start + k * step, start + (k + 1) * step)
            w = (w_high[:, these], w_low[:, these])
        else:
            copy(k).wait()
            w = split(buf[k])
        mixed = dot_split(attended, w)
        at = 0
        for o in outs:
            o[:, columns] = mixed[at : at + o.shape[0]]
            at += o.shape[0]


def mix(operands, ask, rows, keyed, w, kv_width, slots, start, columns, name, step=512):
    q_width, is_split = w[0].shape[0], len(w) == 2
    steps = columns // step
    attended = [jax.ShapeDtypeStruct((rows, q_width), jnp.bfloat16)] * (0 if ask is None else 2)
    out_shape = attended + [jax.ShapeDtypeStruct((s, columns), jnp.float32) for s in slots]
    vmem = pl.BlockSpec(memory_space=pltpu.VMEM)
    scratch = [pltpu.VMEM((steps, q_width, step), jnp.float32), pltpu.SemaphoreType.DMA((steps,))]
    return pl.pallas_call(
        functools.partial(mix_kernel, len(operands), ask, q_width, kv_width, start, step, is_split),
        in_specs=[vmem] * len(operands) + ([vmem] * 2 if is_split else [pl.BlockSpec(memory_space=pl.ANY)]),
        out_specs=[vmem] * len(out_shape),
        out_shape=out_shape,
        scratch_shapes=[] if is_split else scratch,
        compiler_params=pltpu.CompilerParams(vmem_limit_bytes=VMEM_LIMIT),
        cost_estimate=pl.CostEstimate(
            flops=8 * rows * q_width * columns + 32 * rows * keyed * q_width,
            bytes_accessed=4 * columns * (q_width + rows),
            transcendentals=rows * keyed * q_width // HEAD_SIZE_DIM,
        ),
        name=name,
    )(*operands, *w)


def attend_out(parts, first, last, w, kv_width, slots, columns):
    rows = sum(a.shape[0] for a, _ in parts[first:last])
    keyed = sum(a.shape[0] for a, _ in parts)
    flat = [r for pair in parts for r in pair]
    res = mix(flat, slice(first, last), rows, keyed, w, kv_width, slots, 0, columns, "attend_out")
    return res[:2], res[2:]


def out_again(attended, w, slots, start, columns):
    rows = attended[0].shape[0]
    return mix(list(attended), None, rows, 0, w, 0, slots, start, columns, "out_again")


def after(a, *others):
    return lax.optimization_barrier((a, *others))[0]


def cut(sizes):
    return [(sum(sizes[:i]), size) for i, size in enumerate(sizes)]


def on_line_of_four(tokens, w_query, w_key, w_value, w_out):
    rows, depth = tokens.shape
    weights = (w_query, w_key, w_value)
    kv_width = w_key.shape[1]
    halves = cut([depth // 2] * 2)
    last = cut([depth // 2, depth // 4, depth // 4])
    later = (3 * depth // 4, depth // 4)

    def hop(a, pairs):
        return lax.ppermute(a, "col", pairs)

    def swap(a):
        return lax.ppermute(a, "row", CORES)

    def columns(a, start, size):
        return a[:, start : start + size]

    near = hop(tokens, PAIRS)
    mid = [hop(columns(tokens, *h), MIDDLE) for h in halves]
    first = project([((tokens, 0),)], weights, *halves[0])
    mid[0] = after(mid[0], first)
    end2 = [hop(a, ENDS_IN) for a in mid]
    first = project([((tokens, halves[1][0]),)], weights, *halves[1], first, before=mid[:1])
    near = after(near, first)
    mid2 = [hop(columns(near, *halves[0]), MIDDLE)]
    pieces = cut([w_out.shape[1] // 2] * 2)
    w_split = halve(w_out, *pieces[0], near)
    second = third = None
    for (start, size), m, e in zip(halves, mid, end2):
        block = [((near, start),), ((m, 0), (e, 0))]
        second = project(block, weights, start, size, second, before=[w_split[0], mid[1]])
        if start == 0:
            mid2.append(hop(columns(after(near, w_split[0]), *halves[1]), MIDDLE))
            mid2[0] = after(mid2[0], second)
    first, second = [(a, swap(a)) for a in (first, second)]
    for i, (start, size) in enumerate(last):
        half = start // halves[0][1]
        at = start - halves[half][0]
        far = columns(mid2[half], at, size) if size < halves[0][1] else mid2[half]
        if i == 1:
            far = after(far, second[0])
        end3 = hop(far, ENDS_IN)
        block = ((mid2[half], at), (end3, 0))
        if i > 1:
            third = project_last(block, kept, start - later[0], third)
        elif i == 1:
            third = project([block], weights, start, size, third)
        else:
            third, *kept = project([block], weights, start, size, third, later)
    third = (third, swap(third))

    parts = [first, second, third]
    early = cut([pieces[0][1] // 4, 3 * pieces[0][1] // 4, pieces[1][1]])
    a_third, m_third = attend_out(parts, 2, 3, w_split, kv_width, [rows], early[0][1])
    m_third = [m_third[0]] + [
        out_again(a_third, w, [rows], *p)[0] for w, p in zip((w_split, [w_out]), early[1:])
    ]
    r1 = [hop(m, ENDS_OUT) for m in m_third]
    others = [tuple(after(a, r1[0], *m_third) for a in first), second, third]
    a_rest, mixed = attend_out(others, 0, 2, w_split, kv_width, [rows] * 3, pieces[0][1])
    r1[1] = after(r1[1], *a_rest)
    mixed = [mixed, out_again(a_rest, [w_out], [rows] * 3, *pieces[1])]
    far = [jnp.concatenate([m + r for m, r in zip(m_third[:2], r1[:2])], axis=1), m_third[2] + r1[2]]
    result = []
    for (m_own, m_near, m_second), f in zip(mixed, far):
        r2e = hop(m_second, ENDS_OUT)
        r2m = hop(f, MIDDLE)
        r3m = hop(m_second + r2e, MIDDLE)
        r3x = hop(m_near + r2m, PAIRS)
        result.append(m_own + (r3x + r3m))
    return jnp.concatenate(result, axis=1)


def on_device(tokens, w_query, w_key, w_value, w_out):
    highest = lax.Precision.HIGHEST
    gathered = lax.all_gather(tokens, "col", axis=0, tiled=True)
    q_width = w_query.shape[1]
    kv_width = w_key.shape[1]

    def product(weight):
        return jnp.dot(gathered, weight, preferred_element_type=jnp.float32, precision=highest)

    joined = lax.psum_scatter(
        jnp.concatenate([product(w_query), product(w_key), product(w_value)], axis=1),
        "row",
        scatter_dimension=0,
        tiled=True,
    )
    query_rows = joined[:, :q_width]
    keys = lax.all_gather(joined[:, q_width : q_width + kv_width], "row", axis=0, tiled=True)
    values = lax.all_gather(joined[:, q_width + kv_width :], "row", axis=0, tiled=True)
    count_of_rows, count_of_heads = query_rows.shape[0], kv_width // HEAD_SIZE_DIM
    query_rows = query_rows.reshape(count_of_rows, count_of_heads, GROUP, HEAD_SIZE_DIM)
    keys = keys.reshape(-1, count_of_heads, HEAD_SIZE_DIM)
    values = values.reshape(-1, count_of_heads, HEAD_SIZE_DIM)
    scores = jnp.einsum("rkgd,nkd->kgrn", query_rows, keys, precision=highest)
    weights = jax.nn.softmax(scores * (1.0 / math.sqrt(HEAD_SIZE_DIM)), axis=-1)
    attended = jnp.einsum("kgrn,nkd->rkgd", weights, values, precision=highest)
    attended = lax.all_gather(attended.reshape(count_of_rows, q_width), "row", axis=0, tiled=True)
    return lax.psum_scatter(
        jnp.dot(attended, w_out, preferred_element_type=jnp.float32, precision=highest),
        "col",
        scatter_dimension=0,
        tiled=True,
    )


def solution(mesh):
    placed = (
        P(("depth", "col"), "row"),
        P("row", "col"),
        P("row", "col"),
        P("row", "col"),
        P("col", "row"),
    )
    here = mesh.shape["row"] == 2 and mesh.shape["col"] == 4
    return jax.shard_map(
        on_line_of_four if here else on_device,
        mesh=mesh,
        in_specs=placed,
        out_specs=P(("depth", "col"), "row"),
        check_vma=False,
    )
```
